256 devices in a mesh: ctx: 32 (over x, y, z_hi), tp: 8 (over z_lo, core).
Axes of the slice: x: 4, y: 4, z: 8 (z_hi: 2, z_lo: 4; z = z_hi * 4 + z_lo), core: 2. Of those that a mesh axis runs over, the one named last changes fastest.
Arguments:
- medium_input: bfloat16 [8192, 3, 4096], P('ctx', None, 'tp'), may hold values from -6 to 6
- long_input: bfloat16 [8192, 2, 4096], P('ctx', None, 'tp'), may hold values from -6 to 6
- medium_taps: float32 [3, 3, 4096], P(None, None, 'tp'), may hold values from -3.5 to 3.5
- long_taps: float32 [3, 2, 4096], P(None, None, 'tp'), may hold values from -3.5 to 3.5
- medium_filter: bfloat16 [128, 4096], P(None, 'tp'), may hold values from -0.75 to 0.75
- norm_gain: float32 [4096], P('tp'), may hold values from 0.1 to 1.9
- long_residue: float32 [4096, 16], P(('tp', 'ctx')), may hold values from -1.5 to 1.5
- long_log_decay: float32 [4096, 16], P(('tp', 'ctx')), as said below
- cotangent: bfloat16 [8192, 4096], P('ctx', 'tp'), may hold values from -6 to 6
Outputs:
- mixed: bfloat16 [8192, 4096], P('ctx', 'tp')
- grad_medium_input: bfloat16 [8192, 3, 4096], P('ctx', None, 'tp')
- grad_long_input: bfloat16 [8192, 2, 4096], P('ctx', None, 'tp')
- grad_medium_taps: float32 [3, 3, 4096], P(None, None, 'tp')
- grad_long_taps: float32 [3, 2, 4096], P(None, None, 'tp')
- grad_medium_filter: float32 [128, 4096], P(None, 'tp')
- grad_norm_gain: float32 [4096], P('tp')
- grad_long_residue: float32 [4096, 16], P(('tp', 'ctx'))
- grad_long_log_decay: float32 [4096, 16], P(('tp', 'ctx'))
The draws below stay inside these ranges and needn't reach their ends.
Inputs may be any that keep to these rules, and one draw needn't show every extreme that they name: `long_log_decay`: natural logarithm of each mode's decay per base.
All inputs are finite; a program needn't handle non-finite values.
Results may differ from the reference program's by a relative error of at most 0.03.
Values may be sent and summed in bfloat16 or wider, within the bound.
No kernel may reach another device: no remote copies, remote signals or barrier semaphores. Data moves between devices by JAX's collectives and lax.ppermute only.
A program may use at most 128 MiB of HBM per device.

```python
import math
import jax
import jax.numpy as jnp
from jax import lax

D = 4096
FILTER = 128
MODES = 16
TOKENS = 8192


def draw_long_log_decay(key, part):
    key = jax.random.fold_in(key, 11)
    lowest = math.log(0.25 / TOKENS)
    return jax.random.uniform(key, (D, MODES), jnp.float32, lowest, math.log(1.0 / 30.0)).astype(jnp.float32)


def steps_of(stream_key, dims, shards, least, top_value):
    gain, own = 1.0, jax.random.fold_in(stream_key, 6)
    for dim, shards_of in shards:
        draws = jnp.exp(jax.random.uniform(jax.random.fold_in(own, dim), (shards_of,), jnp.float32, least / len(shards), top_value / len(shards)))
        gain = gain * jnp.repeat(draws, dims[dim] // shards_of).reshape([-1 if axis == dim else 1 for axis in range(len(dims))])
    return gain


def scatter_about(stream_key, dims, spread, reach, pieces=(), kind=jnp.bfloat16):
    result = jax.random.normal(stream_key, dims, jnp.float32) * spread
    if len(pieces) > 0:
        result = steps_of(stream_key, dims, pieces, -0.22, 0.18) * result
    return jnp.clip(result, min=-reach, max=reach).astype(kind)


def setup_inputs(seed: int = 0) -> dict:
    seeds = jax.random.split(jax.random.key(seed), 10)
    medium_input = scatter_about(seeds[0], (TOKENS, 3, D), 1.0, 6.0, ((0, 32), (2, 8)))
    long_input = scatter_about(seeds[1], (TOKENS, 2, D), 1.0, 6.0, ((0, 32), (2, 8)))
    medium_taps = scatter_about(seeds[2], (3, 3, D), 3 ** -0.5, 3.5, ((2, 8),), jnp.float32)
    long_taps = scatter_about(seeds[3], (3, 2, D), 3 ** -0.5, 3.5, ((2, 8),), jnp.float32)
    medium_filter = scatter_about(seeds[4], (FILTER, D), 64 ** -0.5, 0.75, ((1, 8),))
    norm_gain = jnp.clip(1.0 + 0.18 * jax.random.normal(seeds[5], (D,), jnp.float32), 0.1, 1.9)
    long_residue = scatter_about(seeds[6], (D, MODES), 0.25, 1.5, ((0, 256),), jnp.float32)
    long_log_decay = draw_long_log_decay(jax.random.fold_in(seeds[9], 71), 0)
    cotangent = scatter_about(seeds[8], (TOKENS, D), 1.0, 6.0, ((0, 32), (1, 8)))
    return {"medium_input": medium_input, "long_input": long_input, "medium_taps": medium_taps, "long_taps": long_taps, "medium_filter": medium_filter, "norm_gain": norm_gain, "long_residue": long_residue, "long_log_decay": long_log_decay, "cotangent": cotangent}


def rounded(values):
    return lax.optimization_barrier(values.astype(jnp.bfloat16)).astype(jnp.float32)

def delayed(values, steps):
    pad_width = ((steps, 0),) + ((0, 0),) * (values.ndim - 1)
    return jnp.pad(values, pad_width)[:values.shape[0]]

def advanced(values, steps):
    pad_width = ((0, steps),) + ((0, 0),) * (values.ndim - 1)
    return jnp.pad(values, pad_width)[steps:]

def featurize(raw_input, taps):
    values = raw_input.astype(jnp.float32)
    return taps[0] * values + taps[1] * delayed(values, 1) + taps[2] * delayed(values, 2)

def unfeaturize(raw_input, taps, grad_feat):
    values = raw_input.astype(jnp.float32)
    grad_raw = taps[0] * grad_feat + taps[1] * advanced(grad_feat, 1) + taps[2] * advanced(grad_feat, 2)
    grad_taps = jnp.stack([lax.optimization_barrier(jnp.sum(grad_feat * values, 0)), lax.optimization_barrier(jnp.sum(grad_feat * delayed(values, 1), 0)), lax.optimization_barrier(jnp.sum(grad_feat * delayed(values, 2), 0))])
    return (grad_raw, grad_taps)

def causal_conv(signal, kernel):
    length = signal.shape[0]
    size_fft = 2 * length
    spectrum = jnp.fft.rfft(signal, size_fft, axis=0) * jnp.fft.rfft(kernel, size_fft, axis=0)
    return jnp.fft.irfft(spectrum, size_fft, axis=0)[:length]

def later_corr(signal, kernel):
    length = signal.shape[0]
    size_fft = 2 * length
    spectrum = jnp.fft.rfft(signal, size_fft, axis=0) * jnp.conj(jnp.fft.rfft(kernel, size_fft, axis=0))
    return jnp.fft.irfft(spectrum, size_fft, axis=0)[:length]

def long_kernel(residue, log_decay, length):
    rate = jnp.exp(log_decay)
    weight = residue * jnp.sqrt(2.0 * rate)
    position = jnp.arange(length, dtype=jnp.int32).astype(jnp.float32)[:, None]
    total = jnp.zeros((length, residue.shape[0]), jnp.float32)
    for index_mode in range(residue.shape[1]):
        total = total + weight[:, index_mode] * jnp.exp(-rate[:, index_mode] * position)
    return total

def long_kernel_back(residue, log_decay, grad_kernel):
    rate = jnp.exp(log_decay)
    root_rate = jnp.sqrt(2.0 * rate)
    position = jnp.arange(grad_kernel.shape[0], dtype=jnp.int32).astype(jnp.float32)[:, None]
    residue_list = []
    decay_list = []
    for index_mode in range(residue.shape[1]):
        decay_curve = jnp.exp(-rate[:, index_mode] * position)
        plain_sum = lax.optimization_barrier(jnp.sum(grad_kernel * decay_curve, 0))
        slope_sum = lax.optimization_barrier(jnp.sum(grad_kernel * decay_curve * (0.5 - rate[:, index_mode] * position), 0))
        residue_list.append(root_rate[:, index_mode] * plain_sum)
        decay_list.append(residue[:, index_mode] * root_rate[:, index_mode] * slope_sum)
    return (jnp.stack(residue_list, 1), jnp.stack(decay_list, 1))

def reference(medium_input, long_input, medium_taps, long_taps, medium_filter, norm_gain, long_residue, long_log_decay, cotangent):
    medium_feat = rounded(featurize(medium_input, medium_taps))
    long_feat = rounded(featurize(long_input, long_taps))
    q_one, k_one, v_one = (medium_feat[:, 0], medium_feat[:, 1], medium_feat[:, 2])
    q_two, k_two = (long_feat[:, 0], long_feat[:, 1])
    prod_one = rounded(k_one * v_one)
    filter_f = medium_filter.astype(jnp.float32)
    conv_one = causal_conv(prod_one, filter_f)
    gated = q_one * conv_one
    scale = lax.rsqrt(lax.optimization_barrier(jnp.mean(gated * gated, axis=1, keepdims=True)) + 1e-06)
    normed = rounded(gated * scale * norm_gain)
    prod_two = rounded(k_two * normed)
    kernel = long_kernel(long_residue, long_log_decay, prod_two.shape[0])
    long_conv = rounded(causal_conv(prod_two, kernel))
    mixed = (q_two * long_conv).astype(jnp.bfloat16)
    grad_out = cotangent.astype(jnp.float32)
    grad_q_two = grad_out * long_conv
    grad_conv = rounded(grad_out * q_two)
    grad_prod_two = rounded(later_corr(grad_conv, kernel))
    grad_kernel = later_corr(grad_conv, prod_two)
    grad_residue, grad_log = long_kernel_back(long_residue, long_log_decay, grad_kernel)
    grad_k_two = grad_prod_two * normed
    grad_normed = grad_prod_two * k_two
    grad_gain = lax.optimization_barrier(jnp.sum(grad_normed * gated * scale, 0))
    weighted = grad_normed * norm_gain
    inner = lax.optimization_barrier(jnp.mean(weighted * gated, axis=1, keepdims=True))
    grad_gated = scale * (weighted - gated * scale * scale * inner)
    grad_conv_one = rounded(grad_gated * q_one)
    grad_q_one = grad_gated * conv_one
    grad_prod_one = later_corr(grad_conv_one, filter_f)
    grad_filter = later_corr(grad_conv_one, prod_one)[:medium_filter.shape[0]]
    grad_k_one = grad_prod_one * v_one
    grad_v_one = grad_prod_one * k_one
    grad_medium, taps_medium = unfeaturize(medium_input, medium_taps, jnp.stack([grad_q_one, grad_k_one, grad_v_one], 1))
    grad_long, taps_long = unfeaturize(long_input, long_taps, jnp.stack([grad_q_two, grad_k_two], 1))
    return (mixed, grad_medium.astype(jnp.bfloat16), grad_long.astype(jnp.bfloat16), taps_medium, taps_long, grad_filter, grad_gain, grad_residue, grad_log)
```

```python
import math

import jax
import jax.numpy as jnp
from jax import lax
from jax.sharding import PartitionSpec as P

D = 4096


precise = lax.Precision.HIGHEST


def passed_along(array, axis, by):
    count = lax.axis_size(axis)
    pairs = [(i, i + by) for i in range(count) if 0 <= i + by < count]
    return lax.ppermute(array, axis, pairs)


def sum_over_tp(column):
    count = lax.axis_size("tp")
    flat = column.reshape(1, -1)
    spread = jnp.broadcast_to(flat, (count, flat.shape[1]))
    gathered = lax.all_to_all(spread, "tp", split_axis=0, concat_axis=0, tiled=True)
    return jnp.sum(gathered, 0).reshape(column.shape)


def sum_over_ctx(rows):
    count = lax.axis_size("ctx")
    total, width = rows.shape
    share = -(-total // count)
    padded = jnp.pad(rows, ((0, share * count - total), (0, 0))).astype(jnp.bfloat16)
    parts = padded.reshape(count, share, width)
    got = lax.all_to_all(parts, "ctx", split_axis=0, concat_axis=0, tiled=True)
    reduced = jnp.sum(got.astype(jnp.float32), 0).astype(jnp.bfloat16)
    spread = jnp.broadcast_to(reduced[None], (count, share, width))
    everyone = lax.all_to_all(spread, "ctx", split_axis=0, concat_axis=0, tiled=True)
    return everyone.reshape(share * count, width)[:total].astype(jnp.float32)


def rounded(values):
    return lax.optimization_barrier(values.astype(jnp.bfloat16)).astype(jnp.float32)


def angles(offset, count_rows, count_cols, period):
    product = (jnp.arange(count_rows, dtype=jnp.int32)[:, None] + offset) * jnp.arange(
        count_cols, dtype=jnp.int32
    )[None, :]
    phase_angle = (product % period).astype(jnp.float32) * (2.0 * math.pi / period)
    return (jnp.cos(phase_angle), jnp.sin(phase_angle))


def featurize(extended, taps):
    values = extended.astype(jnp.float32)
    return taps[0] * values[2:] + taps[1] * values[1:-1] + taps[2] * values[:-2]


def unfeaturize(grad_local, grad_after, extended, taps):
    joined = jnp.concatenate([grad_local, grad_after], 0)
    grad_raw = taps[0] * joined[:-2] + taps[1] * joined[1:-1] + taps[2] * joined[2:]
    values = extended.astype(jnp.float32)
    grad_taps = jnp.stack(
        [
            jnp.sum(grad_local * values[2:], 0),
            jnp.sum(grad_local * values[1:-1], 0),
            jnp.sum(grad_local * values[:-2], 0),
        ]
    )
    return (grad_raw, grad_taps)


def half_spectra(pieces, cos_table, sin_table):
    real_part = jnp.einsum("fp,bpc->bfc", cos_table, pieces, precision=precise)
    imag_part = -jnp.einsum("fp,bpc->bfc", sin_table, pieces, precision=precise)
    return (real_part, imag_part)


def block_rows(real_part, imag_part, cos_table, sin_table):
    return jnp.einsum("mf,bfc->bmc", cos_table, real_part, precision=precise) - jnp.einsum(
        "mf,bfc->bmc", sin_table, imag_part, precision=precise
    )


def fourier_tables(length):
    total = 2 * length
    outer = total // 128
    inner_half = length // 128
    section_cos, section_sin = angles(0, outer, inner_half, outer)
    twist_cos, twist_sin = angles(0, outer, 128, total)
    last_cos, last_sin = angles(0, 128, 128, 128)
    return (
        section_cos,
        section_sin,
        twist_cos[:, :, None],
        twist_sin[:, :, None],
        last_cos,
        last_sin,
    )


def forward_fourier(signal, tables):
    section_cos, section_sin, twist_cos, twist_sin, last_cos, last_sin = tables
    outer, inner_half = section_cos.shape
    channels = signal.shape[1]
    folded = signal.reshape(inner_half, 128 * channels)
    first_re = jnp.dot(section_cos, folded, precision=precise).reshape(outer, 128, channels)
    first_im = -jnp.dot(section_sin, folded, precision=precise).reshape(outer, 128, channels)
    turned_re = first_re * twist_cos + first_im * twist_sin
    turned_im = first_im * twist_cos - first_re * twist_sin
    spec_re = jnp.einsum("kbc,bj->kjc", turned_re, last_cos, precision=precise) + jnp.einsum(
        "kbc,bj->kjc", turned_im, last_sin, precision=precise
    )
    spec_im = jnp.einsum("kbc,bj->kjc", turned_im, last_cos, precision=precise) - jnp.einsum(
        "kbc,bj->kjc", turned_re, last_sin, precision=precise
    )
    return (spec_re, spec_im)


def inverse_fourier(spec_re, spec_im, tables):
    section_cos, section_sin, twist_cos, twist_sin, last_cos, last_sin = tables
    outer, inner_half = section_cos.shape
    channels = spec_re.shape[2]
    back_re = jnp.einsum("kjc,bj->kbc", spec_re, last_cos, precision=precise) - jnp.einsum(
        "kjc,bj->kbc", spec_im, last_sin, precision=precise
    )
    back_im = jnp.einsum("kjc,bj->kbc", spec_im, last_cos, precision=precise) + jnp.einsum(
        "kjc,bj->kbc", spec_re, last_sin, precision=precise
    )
    turned_re = (back_re * twist_cos - back_im * twist_sin).reshape(outer, 128 * channels)
    turned_im = (back_im * twist_cos + back_re * twist_sin).reshape(outer, 128 * channels)
    signal = jnp.dot(section_cos.T, turned_re, precision=precise) - jnp.dot(
        section_sin.T, turned_im, precision=precise
    )
    return (signal / float(outer * 128)).reshape(inner_half * 128, channels)


def long_kernel(residue, log_decay, length):
    rate = jnp.exp(log_decay)
    weight = residue * jnp.sqrt(2.0 * rate)
    position = jnp.arange(length, dtype=jnp.int32).astype(jnp.float32)[:, None]
    total = jnp.zeros((length, residue.shape[0]), jnp.float32)
    for index_mode in range(residue.shape[1]):
        total = total + weight[:, index_mode] * jnp.exp(-rate[:, index_mode] * position)
    return total


def long_kernel_back(residue, log_decay, grad_kernel):
    rate = jnp.exp(log_decay)
    root_rate = jnp.sqrt(2.0 * rate)
    position = jnp.arange(grad_kernel.shape[0], dtype=jnp.int32).astype(jnp.float32)[:, None]
    residue_list = []
    decay_list = []
    for index_mode in range(residue.shape[1]):
        decay_curve = jnp.exp(-rate[:, index_mode] * position)
        plain_sum = jnp.sum(grad_kernel * decay_curve, 0)
        slope_sum = jnp.sum(grad_kernel * decay_curve * (0.5 - rate[:, index_mode] * position), 0)
        residue_list.append(root_rate[:, index_mode] * plain_sum)
        decay_list.append(residue[:, index_mode] * root_rate[:, index_mode] * slope_sum)
    return (jnp.stack(residue_list, 1), jnp.stack(decay_list, 1))


def channel_forward(prod_chan, residue, log_decay):
    length = prod_chan.shape[0]
    tables = fourier_tables(length)
    kernel = long_kernel(residue, log_decay, length)
    prod_re, prod_im = forward_fourier(prod_chan.astype(jnp.float32), tables)
    kern_re, kern_im = forward_fourier(kernel, tables)
    conv_chan = inverse_fourier(
        prod_re * kern_re - prod_im * kern_im, prod_re * kern_im + prod_im * kern_re, tables
    )
    return (conv_chan.astype(jnp.bfloat16), (tables, prod_re, prod_im, kern_re, kern_im))


def channel_backward(grad_chan, saved, residue, log_decay):
    tables, prod_re, prod_im, kern_re, kern_im = saved
    grad_re, grad_im = forward_fourier(grad_chan.astype(jnp.float32), tables)
    back_chan = inverse_fourier(
        grad_re * kern_re + grad_im * kern_im, grad_im * kern_re - grad_re * kern_im, tables
    )
    grad_kernel = inverse_fourier(
        grad_re * prod_re + grad_im * prod_im, grad_im * prod_re - grad_re * prod_im, tables
    )
    grad_residue, grad_log = long_kernel_back(residue, log_decay, grad_kernel)
    return (back_chan.astype(jnp.bfloat16), grad_residue, grad_log)


def on_device(
    medium_input,
    long_input,
    medium_taps,
    long_taps,
    medium_filter,
    norm_gain,
    long_residue,
    long_log_decay,
    cotangent,
):
    tok_rows, chan_width = cotangent.shape
    filter_len = medium_filter.shape[0]
    block_count = tok_rows // filter_len
    packed = jnp.concatenate(
        [
            medium_input[tok_rows - filter_len - 1 :, 1:].reshape(-1, chan_width),
            medium_input[tok_rows - 2 :, :1].reshape(-1, chan_width),
            long_input[tok_rows - 2 :].reshape(-1, chan_width),
        ],
        0,
    )
    before = passed_along(packed, "ctx", 1)
    kv_rows = 2 * (filter_len + 1)
    prev_kv = before[:kv_rows].reshape(filter_len + 1, 2, chan_width)
    prev_q = before[kv_rows : kv_rows + 2].reshape(2, 1, chan_width)
    prev_long = before[kv_rows + 2 :].reshape(2, 2, chan_width)
    ext_kv = jnp.concatenate([prev_kv, medium_input[:, 1:]], 0)
    ext_medium = jnp.concatenate([jnp.concatenate([prev_q, prev_kv[-2:]], 1), medium_input], 0)
    ext_long = jnp.concatenate([prev_long, long_input], 0)
    feat_kv = rounded(featurize(ext_kv, medium_taps[:, 1:]))
    q_one = rounded(featurize(ext_medium[:, :1], medium_taps[:, :1]))[:, 0]
    feat_long = rounded(featurize(ext_long, long_taps))
    q_two = feat_long[:, 0]
    k_two = feat_long[:, 1]
    key_ext = feat_kv[:, 0]
    val_ext = feat_kv[:, 1]
    key_loc = key_ext[filter_len - 1 :]
    val_loc = val_ext[filter_len - 1 :]
    prod_one = rounded(key_ext * val_ext)
    padded = jnp.concatenate([jnp.zeros((1, chan_width), jnp.float32), prod_one], 0).reshape(
        block_count + 1, filter_len, chan_width
    )
    cos_full, sin_full = angles(0, 2 * filter_len, 2 * filter_len, 2 * filter_len)
    cos_lo, sin_lo = (cos_full[:, :filter_len], sin_full[:, :filter_len])
    cos_hi, sin_hi = (cos_full[:, filter_len:], sin_full[:, filter_len:])
    top_cos, top_sin = angles(filter_len, filter_len, 2 * filter_len, 2 * filter_len)
    low_cos, low_sin = angles(0, filter_len, 2 * filter_len, 2 * filter_len)
    top_cos, top_sin = (top_cos / (2.0 * filter_len), top_sin / (2.0 * filter_len))
    low_cos, low_sin = (low_cos / (2.0 * filter_len), low_sin / (2.0 * filter_len))
    lo_re, lo_im = half_spectra(padded[:-1], cos_lo, sin_lo)
    hi_re, hi_im = half_spectra(padded[1:], cos_hi, sin_hi)
    win_re = lo_re + hi_re
    win_im = lo_im + hi_im
    filter_f = medium_filter.astype(jnp.float32)
    ker_re = jnp.dot(cos_lo, filter_f, precision=precise)
    ker_im = -jnp.dot(sin_lo, filter_f, precision=precise)
    conv_one = block_rows(
        win_re * ker_re - win_im * ker_im, win_re * ker_im + win_im * ker_re, top_cos, top_sin
    ).reshape(tok_rows, chan_width)
    gated = q_one * conv_one
    square_sum = sum_over_tp(jnp.sum(gated * gated, 1, keepdims=True))
    scale = lax.rsqrt(square_sum / D + 1e-06)
    normed = rounded(gated * scale * norm_gain)
    prod_two = (k_two * normed).astype(jnp.bfloat16)
    grad_out = cotangent.astype(jnp.float32)
    grad_conv = (grad_out * q_two).astype(jnp.bfloat16)
    prod_chan = lax.all_to_all(prod_two, "ctx", split_axis=1, concat_axis=0, tiled=True)
    conv_chan, saved = channel_forward(prod_chan, long_residue, long_log_decay)
    long_conv = lax.all_to_all(conv_chan, "ctx", split_axis=0, concat_axis=1, tiled=True)
    grad_chan = lax.all_to_all(grad_conv, "ctx", split_axis=1, concat_axis=0, tiled=True)
    back_chan, grad_residue, grad_log = channel_backward(
        grad_chan, saved, long_residue, long_log_decay
    )
    grad_prod_two = lax.all_to_all(back_chan, "ctx", split_axis=0, concat_axis=1, tiled=True)
    conv_f = long_conv.astype(jnp.float32)
    mixed = (q_two * conv_f).astype(jnp.bfloat16)
    grad_q_two = grad_out * conv_f
    grad_prod_f = grad_prod_two.astype(jnp.float32)
    grad_k_two = grad_prod_f * normed
    grad_normed = grad_prod_f * k_two
    gain_local = jnp.sum(grad_normed * gated * scale, 0)
    weighted = grad_normed * norm_gain
    inner_sum = sum_over_tp(jnp.sum(weighted * gated, 1, keepdims=True))
    grad_gated = scale * (weighted - gated * scale * scale * (inner_sum / D))
    grad_conv_one = rounded(grad_gated * q_one)
    grad_q_one = grad_gated * conv_one
    head_rows = jnp.stack(
        [
            jnp.sum(filter_f * grad_conv_one[shift_rows : shift_rows + filter_len], 0)
            for shift_rows in range(2)
        ]
    )
    head_medium = jnp.stack([grad_q_one[:2], head_rows * val_loc[:2], head_rows * key_loc[:2]], 1)
    head_long = jnp.stack([grad_q_two[:2], grad_k_two[:2]], 1)
    packed_back = jnp.concatenate(
        [
            grad_conv_one[: filter_len - 1],
            head_medium.reshape(-1, chan_width),
            head_long.reshape(-1, chan_width),
        ],
        0,
    )
    after = passed_along(packed_back.astype(jnp.bfloat16), "ctx", -1).astype(packed_back.dtype)
    next_conv = after[: filter_len - 1]
    next_medium = after[filter_len - 1 : filter_len + 5].reshape(2, 3, chan_width)
    next_long = after[filter_len + 5 :].reshape(2, 2, chan_width)
    grad_pad = jnp.concatenate(
        [grad_conv_one, next_conv, jnp.zeros((1, chan_width), jnp.float32)], 0
    ).reshape(block_count + 1, filter_len, chan_width)
    glo_re, glo_im = half_spectra(grad_pad[:-1], cos_lo, sin_lo)
    ghi_re, ghi_im = half_spectra(grad_pad, cos_hi, sin_hi)
    gwin_re = glo_re + ghi_re[1:]
    gwin_im = glo_im + ghi_im[1:]
    grad_prod_one = block_rows(
        gwin_re * ker_re + gwin_im * ker_im, gwin_im * ker_re - gwin_re * ker_im, low_cos, low_sin
    ).reshape(tok_rows, chan_width)
    dpos_re = ghi_re[:-1]
    dpos_im = ghi_im[:-1]
    cross_re = jnp.sum(dpos_re * win_re + dpos_im * win_im, 0)
    cross_im = jnp.sum(dpos_im * win_re - dpos_re * win_im, 0)
    grad_filter = jnp.dot(low_cos, cross_re, precision=precise) - jnp.dot(
        low_sin, cross_im, precision=precise
    )
    grad_k_one = grad_prod_one * val_loc
    grad_v_one = grad_prod_one * key_loc
    grad_medium, taps_medium = unfeaturize(
        jnp.stack([grad_q_one, grad_k_one, grad_v_one], 1), next_medium, ext_medium, medium_taps
    )
    grad_long, taps_long = unfeaturize(
        jnp.stack([grad_q_two, grad_k_two], 1), next_long, ext_long, long_taps
    )
    summed = sum_over_ctx(
        jnp.concatenate(
            [
                grad_filter,
                taps_medium.reshape(9, chan_width),
                taps_long.reshape(6, chan_width),
                gain_local[None],
            ],
            0,
        )
    )
    grad_filter = summed[:filter_len]
    taps_medium = summed[filter_len : filter_len + 9].reshape(3, 3, chan_width)
    taps_long = summed[filter_len + 9 : filter_len + 15].reshape(3, 2, chan_width)
    gain_total = summed[filter_len + 15]
    return (
        mixed,
        grad_medium.astype(jnp.bfloat16),
        grad_long.astype(jnp.bfloat16),
        taps_medium,
        taps_long,
        grad_filter,
        gain_total,
        grad_residue,
        grad_log,
    )


def solution(mesh):
    return jax.shard_map(
        on_device,
        mesh=mesh,
        in_specs=(
            P("ctx", None, "tp"),
            P("ctx", None, "tp"),
            P(None, None, "tp"),
            P(None, None, "tp"),
            P(None, "tp"),
            P("tp"),
            P(("tp", "ctx"), None),
            P(("tp", "ctx"), None),
            P("ctx", "tp"),
        ),
        out_specs=(
            P("ctx", "tp"),
            P("ctx", None, "tp"),
            P("ctx", None, "tp"),
            P(None, None, "tp"),
            P(None, None, "tp"),
            P(None, "tp"),
            P("tp"),
            P(("tp", "ctx"), None),
            P(("tp", "ctx"), None),
        ),
        check_vma=False,
    )
```

```python
import functools
import math

import jax
import jax.numpy as jnp
import ml_dtypes
import numpy as np
from jax import lax
from jax.experimental import pallas as pl
from jax.experimental.pallas import tpu as pltpu
from jax.sharding import PartitionSpec as P

D = 4096
MODES = 16
TAPS = 128
ROWS = 256
LANES = 128
CHUNKS = 8
STEPS = ROWS // CHUNKS
HALO = 144
SHARE = 5
LIMIT = 60
F32 = jnp.float32
BF16 = jnp.bfloat16
precise = lax.Precision.HIGHEST


def fourier_matrices():
    size = 2 * TAPS
    place = np.arange(size)
    mode = np.arange(TAPS)
    turn = 2.0 * math.pi / size
    cos_part = np.cos(turn * ((mode[:, None] * place[None, :]) % size))
    sin_part = -np.sin(turn * ((mode[:, None] * place[None, :]) % size))
    sin_part[0] = 1.0 - 2.0 * (place % 2)
    forward = np.concatenate([cos_part, sin_part], 0)
    weight = np.full((size,), 2.0 / size)
    weight[0] = weight[TAPS] = 1.0 / size
    backward = (forward * weight[:, None]).T

    def halves(table):
        high = table.astype(ml_dtypes.bfloat16)
        low = (table - high.astype(np.float64)).astype(ml_dtypes.bfloat16)
        return np.concatenate([high, low], 0)

    return halves(forward), halves(backward[:TAPS]), halves(backward[TAPS:])


def f32_of(value):
    return value.astype(F32)


def rounded(value):
    return value.astype(BF16).astype(F32)


def spectrum(table, signal):
    both = jnp.dot(table, signal, preferred_element_type=F32)
    return both[: 2 * TAPS] + both[2 * TAPS :]


def from_spectrum(table, values):
    high = values.astype(BF16)
    low = (values - high.astype(F32)).astype(BF16)
    both = jnp.dot(table, high, preferred_element_type=F32)
    rest = jnp.dot(table[:TAPS], low, preferred_element_type=F32)
    return both[:TAPS] + both[TAPS:] + rest


def split_spectrum(values):
    real, imag = values[:TAPS], values[TAPS:]
    first = lax.broadcasted_iota(jnp.int32, real.shape, 0) == 0
    return real, jnp.where(first, imag, real), jnp.where(first, 0.0, imag)


def spread(value, row):
    return jnp.broadcast_to(value[row : row + 1, :], (CHUNKS, LANES))


def chunk_index():
    return lax.broadcasted_iota(jnp.int32, (CHUNKS, LANES), 0)


def at_step(ref, step):
    return ref[pl.ds(step, CHUNKS, stride=STEPS), :]


def chunk_states(source, rate, backward):
    decay = jnp.exp(-rate)
    decays = [spread(decay, r) for r in range(MODES)]

    def body(n, states):
        value = at_step(source, STEPS - 1 - n if backward else n)
        return tuple(decays[r] * states[r] + value for r in range(MODES))

    first = at_step(source, 0)
    return lax.fori_loop(0, STEPS, body, (first - first,) * MODES, unroll=4)


def chunk_entries(ends, rate, backward):
    place = chunk_index()
    entries = []
    for r in range(MODES):
        total = ends[r]
        rate_r = spread(rate, r)
        for by in (1, 2, 4):
            factor = jnp.exp(rate_r * float(-STEPS * by))
            moved = pltpu.roll(total, CHUNKS - by if backward else by, 0)
            inside = place < CHUNKS - by if backward else place >= by
            total = total + jnp.where(inside, factor * moved, 0.0)
        moved = pltpu.roll(total, CHUNKS - 1 if backward else 1, 0)
        entries.append(jnp.where(place < CHUNKS - 1 if backward else place >= 1, moved, 0.0))
    return entries


def chunk_weights(rate, r, backward):
    place = chunk_index()
    after = (place if backward else CHUNKS - 1 - place).astype(F32) * float(STEPS)
    return jnp.exp(-spread(rate, r) * after), after


def local_answer(source, target, rate, weight, entries, backward):
    decay = jnp.exp(-rate)
    decays = [spread(decay, r) for r in range(MODES)]
    weights = [spread(weight, r) for r in range(MODES)]

    def body(n, states):
        step = STEPS - 1 - n if backward else n
        value = at_step(source, step)
        states = tuple(decays[r] * states[r] + value for r in range(MODES))
        terms = [weights[r] * states[r] for r in range(MODES)]
        while len(terms) > 1:
            terms = [terms[k] + terms[k + 1] for k in range(0, len(terms), 2)]
        target[pl.ds(step, CHUNKS, stride=STEPS), :] = terms[0]
        return states

    lax.fori_loop(0, STEPS, body, tuple(entries), unroll=2)


def add_entry(local, target, rate, weight, entry, backward):
    decay = jnp.exp(-rate)
    decays = [spread(decay, r) for r in range(MODES)]
    start = weight * entry
    place = chunk_index()
    ahead = (CHUNKS - 1 - place if backward else place).astype(F32) * float(STEPS)
    parts = [spread(start, r) * jnp.exp(-spread(rate, r) * ahead) for r in range(MODES)]

    def body(n, parts):
        step = STEPS - 1 - n if backward else n
        parts = tuple(decays[r] * parts[r] for r in range(MODES))
        terms = list(parts)
        while len(terms) > 1:
            terms = [terms[k] + terms[k + 1] for k in range(0, len(terms), 2)]
        target[pl.ds(step, CHUNKS, stride=STEPS), :] = at_step(local, step) + terms[0]
        return parts

    lax.fori_loop(0, STEPS, body, tuple(parts), unroll=4)


def entry_state(gathered, rate, count, backward):
    far = jnp.exp(rate * float(-ROWS))

    def body(n, state):
        device = gathered.shape[0] - 1 - n if backward else n
        return far * state + gathered[device, 0:MODES, :].astype(F32)

    return lax.fori_loop(0, count, body, jnp.zeros((MODES, LANES), F32))


def extend(ext, before, body):
    ext[6:8, :] = before
    ext[8 : 8 + ROWS, :] = body


def three(ext, taps):
    return (
        taps[0:1] * ext[8 : 8 + ROWS, :]
        + taps[1:2] * ext[7 : 7 + ROWS, :]
        + taps[2:3] * ext[6 : 6 + ROWS, :]
    )


def store_tap_sums(target, row, grad, ext):
    for shift in range(3):
        target[row + shift : row + shift + 1, :] = jnp.sum(
            grad * ext[8 - shift : 8 - shift + ROWS, :], 0, keepdims=True
        )


def tail_kernel(med, lng, taps, out, ext, rows):
    def feature(j):
        extend(ext, jnp.zeros((2, LANES), F32), f32_of(med[j]))
        return rounded(three(ext, taps[j]))

    key = feature(1)
    val = feature(2)
    out[0:TAPS, :] = (key[TAPS:] * val[TAPS:]).astype(BF16)
    rows[...] = jnp.zeros(rows.shape, F32)
    for j in range(3):
        ext[8 : 8 + ROWS, :] = f32_of(med[j])
        rows[2 * j : 2 * j + 2, :] = ext[6 + ROWS : 8 + ROWS, :]
    for j in range(2):
        ext[8 : 8 + ROWS, :] = f32_of(lng[j])
        rows[6 + 2 * j : 8 + 2 * j, :] = ext[6 + ROWS : 8 + ROWS, :]
    out[TAPS:HALO, :] = rows[...].astype(BF16)


def long_kernel(packed, before, lng, taps, cot, rate_out, weight_out, q_out, k_out, g_out, z_out, ext, halo, grad, rows):
    both = jnp.transpose(packed[...].reshape(LANES, LANES))
    rate = jnp.exp(both[:MODES])
    rate_out[...] = rate
    weight_out[...] = both[MODES : 2 * MODES] * jnp.sqrt(2.0 * rate)
    halo[...] = f32_of(before[...])
    feats = []
    for j in range(2):
        extend(ext, halo[TAPS + 6 + 2 * j : TAPS + 8 + 2 * j, :], f32_of(lng[j]))
        feats.append(three(ext, taps[j]).astype(BF16))
    q_out[...] = feats[0]
    k_out[...] = feats[1]
    sent = (f32_of(cot[...]) * f32_of(feats[0])).astype(BF16)
    g_out[...] = sent
    grad[...] = f32_of(sent)
    states = chunk_states(grad, rate, True)
    for r in range(MODES):
        factor, _ = chunk_weights(rate, r, True)
        rows[r : r + 1, :] = jnp.sum(factor * states[r], 0, keepdims=True)
    z_out[...] = jnp.broadcast_to(rows[...].astype(BF16)[None], z_out.shape)


def medium_kernel(med, before, taps, filt, forward, top, gconv, rate, weight,
                  prod_out, q_out, k_out, v_out, conv_out, gated_out, sq_out, y_out, ext, halo, grad):
    halo[...] = f32_of(before[...])
    feats = []
    for j in range(3):
        extend(ext, halo[TAPS + 2 * j : TAPS + 2 * j + 2, :], f32_of(med[j]))
        feats.append(three(ext, taps[j]).astype(BF16))
    q_out[...] = feats[0]
    k_out[...] = feats[1]
    v_out[...] = feats[2]
    prod_out[0:TAPS, :] = before[0:TAPS, :]
    prod_out[TAPS:, :] = (f32_of(feats[1]) * f32_of(feats[2])).astype(BF16)
    windows = jnp.concatenate([prod_out[0 : 2 * TAPS, :], prod_out[TAPS:, :]], 1)
    win = spectrum(forward[...], windows)
    ker = spectrum(forward[:, 0:TAPS], filt[...])
    ker_re, ker_alt, ker_im = split_spectrum(ker)
    ker_re, ker_alt, ker_im = (jnp.concatenate([k, k], 1) for k in (ker_re, ker_alt, ker_im))
    re, im = win[:TAPS], win[TAPS:]
    spec = jnp.concatenate([re * ker_re - im * ker_im, im * ker_alt + re * ker_im], 0)
    answer = from_spectrum(top[...], spec)
    conv = jnp.concatenate([answer[:, :LANES], answer[:, LANES:]], 0)
    conv_out[...] = conv
    gated = f32_of(feats[0]) * conv
    gated_out[...] = gated
    part = lax.dot_general(
        jnp.ones((8, LANES), F32), gated * gated, (((1,), (1,)), ((), ())),
        precision=precise, preferred_element_type=F32,
    )

    @pl.when(pl.program_id(0) == 0)
    def _():
        sq_out[...] = jnp.zeros(sq_out.shape, F32)

    sq_out[...] += part
    grad[...] = f32_of(gconv[...])
    ends = chunk_states(grad, rate[...], True)
    entries = chunk_entries(ends, rate[...], True)
    local_answer(grad, y_out, rate[...], weight[...], entries, True)


def inner_kernel(me, zg, rate, weight, y_loc, k_two, gated, gain, gp_out, zin_out, in_out, full):
    entry = entry_state(zg, rate[...], zg.shape[0] - 1 - me[0], True)
    zin_out[...] = entry
    add_entry(y_loc, full, rate[...], weight[...], entry, True)
    sent = full[...].astype(BF16)
    gp_out[...] = sent
    product = f32_of(sent) * f32_of(k_two[...]) * gain[...] * gated[...]
    part = lax.dot_general(
        jnp.ones((8, LANES), F32), product, (((1,), (1,)), ((), ())),
        precision=precise, preferred_element_type=F32,
    )

    @pl.when(pl.program_id(0) == 0)
    def _():
        in_out[...] = jnp.zeros(in_out.shape, F32)

    in_out[...] += part


def norm_kernel(sums, gated, conv, q_one, k_one, v_one, k_two, gp, gain, filt, cot,
                x_out, gco_out, gq1_out, gk2_out, gain_out, e_out, work, tail):
    ones = jnp.ones((8, LANES), F32)

    def column(values):
        return lax.dot_general(
            values, ones, (((0,), (0,)), ((), ())), precision=precise, preferred_element_type=F32
        )

    square = column(sums[:, 0:ROWS]) / float(D) + 1e-06
    inner = column(sums[:, ROWS:]) / float(D)
    scale = lax.rsqrt(square)
    gate = gated[...]
    key_two = f32_of(k_two[...])
    normed = rounded(gate * scale * gain[...])
    prod_two = (key_two * normed).astype(BF16)
    x_out[...] = prod_two
    grad_two = f32_of(gp[...])
    grad_k_two = grad_two * normed
    gk2_out[...] = grad_k_two
    grad_normed = grad_two * key_two
    gain_out[...] = jnp.broadcast_to(jnp.sum(grad_normed * gate * scale, 0, keepdims=True), gain_out.shape)
    grad_gated = scale * (grad_normed * gain[...] - gate * scale * scale * inner)
    grad_q_one = grad_gated * conv[...]
    gq1_out[...] = grad_q_one
    gco = (grad_gated * f32_of(q_one[...])).astype(BF16)
    gco_out[...] = gco
    e_out[0:TAPS, :] = gco[0:TAPS]
    tail[...] = jnp.zeros(tail.shape, F32)
    tail[0:2, :] = grad_q_one[0:2]
    work[...] = f32_of(gco)
    taps = f32_of(filt[...])
    for shift in range(2):
        head = jnp.sum(taps * work[shift : shift + TAPS, :], 0, keepdims=True)
        tail[2 + shift : 3 + shift, :] = head * f32_of(v_one[0:16, :])[shift : shift + 1]
        tail[4 + shift : 5 + shift, :] = head * f32_of(k_one[0:16, :])[shift : shift + 1]
    tail[6:8, :] = grad_k_two[0:2]
    tail[8:10, :] = f32_of(prod_two)[0:2]
    tail[10:12, :] = f32_of(cot[0:16, :])[0:2]
    e_out[TAPS:HALO, :] = tail[...].astype(BF16)


def filter_kernel(x, gco, gq1, gk2, gain, prod, med, lng, before, rate, forward, low, slot_out, ext, halo, f_out, work, slot):
    halo[...] = f32_of(before[...])
    work[...] = f32_of(x[...])
    states = chunk_states(work, rate[...], False)
    for r in range(MODES):
        factor, _ = chunk_weights(rate[...], r, False)
        slot[r : r + 1, :] = jnp.sum(factor * states[r], 0, keepdims=True)
    f_out[TAPS:, :] = jnp.zeros((f_out.shape[0] - TAPS, LANES), F32)
    f_out[TAPS : TAPS + 1, :] = gain[0:1, :]
    extend(ext, halo[TAPS : TAPS + 2, :], f32_of(med[0]))
    store_tap_sums(f_out, TAPS + 1, gq1[...], ext)
    extend(ext, halo[TAPS + 8 : TAPS + 10, :], f32_of(lng[1]))
    store_tap_sums(f_out, TAPS + 4, gk2[...], ext)
    windows = jnp.concatenate([prod[0 : 2 * TAPS, :], prod[TAPS:, :]], 1)
    win = spectrum(forward[...], windows)
    pieces = jnp.concatenate([gco[0:TAPS, :], gco[TAPS:, :]], 1)
    grd = spectrum(forward[:, TAPS:], pieces)
    win_re, win_alt, win_im = split_spectrum(win)
    re, im = grd[:TAPS], grd[TAPS:]
    spec = jnp.concatenate([re * win_re + im * win_im, im * win_alt - re * win_im], 0)
    f_out[0:TAPS, :] = from_spectrum(low[...], spec[:, :LANES] + spec[:, LANES:])
    for device in range(slot_out.shape[0]):
        slot[MODES:, :] = f_out[SHARE * device : SHARE * device + 8, :]
        slot_out[device] = slot[...].astype(BF16)


def behind_kernel(g, rate, ends_out, gs):
    gs[...] = f32_of(g[...])
    decay = jnp.exp(-rate[...])
    first = at_step(gs, 0)
    zero = first - first
    half = MODES // 2
    for base in range(0, MODES, half):
        decays = [spread(decay, base + r) for r in range(half)]

        def behind(n, carry):
            z, q = carry
            grad = at_step(gs, STEPS - 1 - n)
            q = tuple(decays[r] * (q[r] + z[r]) for r in range(half))
            z = tuple(decays[r] * z[r] + grad for r in range(half))
            return z, q

        z, q = lax.fori_loop(0, STEPS, behind, ((zero,) * half,) * 2, unroll=4)
        for r in range(half):
            ends_out[base + r] = z[r]
            ends_out[MODES + base + r] = q[r]


def modes_kernel(x, g, rate, weight, ends, y_out, sums_out, xs, gs):
    xs[...] = f32_of(x[...])
    gs[...] = f32_of(g[...])
    rates = rate[...]
    decay = jnp.exp(-rates)
    first = at_step(xs, 0)
    zero = first - first
    half = MODES // 2
    s_end, q_end, plain, slope = [], [], [], []
    for base in range(0, MODES, half):
        decays = [spread(decay, base + r) for r in range(half)]

        def ahead(n, carry):
            s, q, p, l = carry
            value, grad = at_step(xs, n), at_step(gs, n)
            q = tuple(decays[r] * (q[r] + s[r]) for r in range(half))
            s = tuple(decays[r] * s[r] + value for r in range(half))
            p = tuple(p[r] + grad * s[r] for r in range(half))
            l = tuple(l[r] + grad * q[r] for r in range(half))
            return s, q, p, l

        s, q, p, l = lax.fori_loop(0, STEPS, ahead, ((zero,) * half,) * 4, unroll=4)
        s_end += s
        q_end += q
        plain += p
        slope += l
    z_end = [ends[r] for r in range(MODES)]
    zq_end = [ends[MODES + r] for r in range(MODES)]
    entries = chunk_entries(s_end, rates, False)
    exits = chunk_entries(z_end, rates, True)
    for r in range(MODES):
        a = spread(decay, r)
        a_step = jnp.exp(spread(rates, r) * float(-STEPS - 1))
        one = plain[r] + entries[r] * a * z_end[r]
        two = (
            slope[r]
            + float(STEPS) * a_step * entries[r] * exits[r]
            + a * (entries[r] * zq_end[r] + exits[r] * (q_end[r] + s_end[r]))
        )
        back, back_steps = chunk_weights(rates, r, True)
        front, front_steps = chunk_weights(rates, r, False)
        rows = (
            one,
            two,
            back * z_end[r],
            back * (zq_end[r] + back_steps * z_end[r]),
            front * (q_end[r] + s_end[r] + front_steps * s_end[r]),
        )
        for kind, value in enumerate(rows):
            place = kind * MODES + r
            sums_out[place : place + 1, :] = jnp.sum(value, 0, keepdims=True)
    local_answer(xs, y_out, rates, weight[...], entries, False)


def answer_kernel(me, sg, rate, weight, y_loc, q_two, cot, sums, zin, after, gco, filt, k_one, v_one, med, lng, before,
                  forward, low, mixed_out, gq2_out, gk1_out, gv1_out, res_out, taps_out, next_out, ext, halo, full, tail):
    rates = rate[...]
    entry = entry_state(sg, rates, me[0], False)
    add_entry(y_loc, full, rates, weight[...], entry, False)
    conv = rounded(full[...])
    grad_out = f32_of(cot[...])
    mixed_out[...] = (f32_of(q_two[...]) * conv).astype(BF16)
    grad_q_two = grad_out * conv
    gq2_out[...] = grad_q_two
    tail[...] = f32_of(after[TAPS:HALO, :])
    decay = jnp.exp(-rates)
    exit_state = jnp.exp(rates * float(-ROWS)) * entry + f32_of(sg[me[0], 0:MODES, :])
    next_out[...] = jnp.zeros(next_out.shape, F32)
    state = exit_state
    for step in range(2):
        state = decay * state + tail[8 + step : 9 + step, :]
        value = rounded(jnp.sum(weight[...] * state, 0, keepdims=True))
        next_out[step : step + 1, :] = value * tail[10 + step : 11 + step, :]
    plain = sums[0:MODES, :] + entry * decay * sums[2 * MODES : 3 * MODES, :]
    slope = (
        sums[MODES : 2 * MODES, :]
        + float(ROWS) * jnp.exp(rates * float(-ROWS - 1)) * entry * zin[...]
        + decay * (entry * sums[3 * MODES : 4 * MODES, :] + zin[...] * sums[4 * MODES :, :])
    )
    res_out[0:MODES, :] = jnp.sqrt(2.0 * rates) * plain
    res_out[MODES:, :] = weight[...] * (0.5 * plain - rates * slope)
    pieces = jnp.concatenate(
        [gco[...], jnp.concatenate([gco[TAPS:, :], after[0:TAPS, :]], 0)], 1
    )
    win = spectrum(forward[...], pieces)
    ker = spectrum(forward[:, 0:TAPS], filt[...])
    ker_re, ker_alt, ker_im = (jnp.concatenate([k, k], 1) for k in split_spectrum(ker))
    re, im = win[:TAPS], win[TAPS:]
    spec = jnp.concatenate([re * ker_re + im * ker_im, im * ker_alt - re * ker_im], 0)
    answer = from_spectrum(low[...], spec)
    grad_prod = jnp.concatenate([answer[:, :LANES], answer[:, LANES:]], 0)
    grad_k = grad_prod * f32_of(v_one[...])
    grad_v = grad_prod * f32_of(k_one[...])
    gk1_out[...] = grad_k
    gv1_out[...] = grad_v
    halo[...] = f32_of(before[...])
    taps_out[...] = jnp.zeros(taps_out.shape, F32)
    extend(ext, halo[TAPS + 2 : TAPS + 4, :], f32_of(med[1]))
    store_tap_sums(taps_out, 0, grad_k, ext)
    extend(ext, halo[TAPS + 4 : TAPS + 6, :], f32_of(med[2]))
    store_tap_sums(taps_out, 3, grad_v, ext)
    extend(ext, halo[TAPS + 6 : TAPS + 8, :], f32_of(lng[0]))
    store_tap_sums(taps_out, 6, grad_q_two, ext)


def input_kernel(gq1, gk1, gv1, gq2, gk2, after, nxt, mtaps, ltaps, med_out, lng_out, ext, tail):
    tail[...] = f32_of(after[TAPS:HALO, :])

    def back(grad, following, taps):
        ext[0:ROWS, :] = grad[...]
        ext[ROWS : ROWS + 2, :] = following
        return (
            taps[0:1] * ext[0:ROWS, :] + taps[1:2] * ext[1 : ROWS + 1, :] + taps[2:3] * ext[2 : ROWS + 2, :]
        ).astype(BF16)

    med_out[0] = back(gq1, tail[0:2, :], mtaps[0])
    med_out[1] = back(gk1, tail[2:4, :], mtaps[1])
    med_out[2] = back(gv1, tail[4:6, :], mtaps[2])
    lng_out[0] = back(gq2, nxt[0:2, :], ltaps[0])
    lng_out[1] = back(gk2, tail[6:8, :], ltaps[1])


def finish_kernel(last, mtap_out, ltap_out, filt_out, gain_out, res_out, log_out, f_all):
    added = jnp.zeros((last.shape[1], LANES), F32)
    for device in range(last.shape[0]):
        piece = f32_of(last[device])
        f_all[SHARE * device : SHARE * device + 8, :] = piece[0:8]
        added = added + piece
    filt_out[...] = f_all[0:TAPS, :]
    gain_out[...] = f_all[TAPS : TAPS + 1, :]
    for shift in range(3):
        mtap_out[shift, 0:1, :] = f_all[TAPS + 1 + shift : TAPS + 2 + shift, :]
        ltap_out[shift, 1:2, :] = f_all[TAPS + 4 + shift : TAPS + 5 + shift, :]
        mtap_out[shift, 1:2, :] = added[SHARE + shift : SHARE + 1 + shift]
        mtap_out[shift, 2:3, :] = added[SHARE + 3 + shift : SHARE + 4 + shift]
        ltap_out[shift, 0:1, :] = added[SHARE + 6 + shift : SHARE + 7 + shift]
    block = pl.program_id(0)
    lane = lax.broadcasted_iota(jnp.int32, (MODES, LANES), 1)
    row = lax.broadcasted_iota(jnp.int32, (MODES, LANES), 0)
    picked = jnp.where(lane % MODES == row, added[SHARE + 9 : SHARE + 10], 0.0)
    goal = (row == lane // MODES + 8 * (block % 2)).astype(F32)
    part = lax.dot_general(
        picked, goal, (((1,), (1,)), ((), ())), precision=precise, preferred_element_type=F32
    )

    @pl.when(block == 0)
    def _():
        res_out[...] = part

    @pl.when(block == 1)
    def _():
        res_out[...] += part

    @pl.when(block == 2)
    def _():
        log_out[...] = part

    @pl.when(block == 3)
    def _():
        log_out[...] += part


def block_of(shape, kind):
    if kind in ("lane", "kept"):
        lead = shape[:-1]
        return pl.BlockSpec(lead + (LANES,), lambda l: (0,) * len(lead) + (l,))
    if kind == "whole":
        return pl.BlockSpec(shape, lambda l: (0,) * len(shape))
    if kind == "source":
        return pl.BlockSpec((8,) + shape[1:], lambda l: (l,) + (0,) * (len(shape) - 1))
    return pl.BlockSpec(memory_space=pltpu.SMEM)


def run(kernel, name, width, inputs, outputs, scratch, flops=1000000):
    arrays = [array for array, _ in inputs]
    moved = sum(a.size * a.dtype.itemsize for a in arrays)
    return pl.pallas_call(
        kernel,
        grid=(width // LANES,),
        in_specs=[block_of(a.shape, kind) for a, kind in inputs],
        out_specs=[block_of(shape, kind) for shape, _, kind in outputs],
        out_shape=[
            pltpu.VMEM(shape, dtype) if kind == "kept" else jax.ShapeDtypeStruct(shape, dtype)
            for shape, dtype, kind in outputs
        ],
        scratch_shapes=[pltpu.VMEM(shape, F32) for shape in scratch],
        compiler_params=pltpu.CompilerParams(vmem_limit_bytes=LIMIT * 1024 * 1024),
        cost_estimate=pl.CostEstimate(flops=flops, bytes_accessed=moved, transcendentals=0),
        name=name,
    )(*arrays)


def passed_along(array, axis, by):
    count = lax.axis_size(axis)
    pairs = [(i, i + by) for i in range(count) if 0 <= i + by < count]
    return lax.ppermute(array, axis, pairs)


def swap(array, axis):
    return lax.all_to_all(array, axis, split_axis=0, concat_axis=0, tiled=True)


def on_device(medium_input, long_input, medium_taps, long_taps, medium_filter, norm_gain, long_residue, long_log_decay, cotangent):
    width = cotangent.shape[1]
    count = lax.axis_size("ctx")
    me = lax.axis_index("ctx").astype(jnp.int32).reshape(1)
    forward, low, top = (jnp.asarray(table) for table in fourier_matrices())
    med = jnp.transpose(medium_input, (1, 0, 2))
    lng = jnp.transpose(long_input, (1, 0, 2))
    mtaps = jnp.transpose(medium_taps, (1, 0, 2))
    ltaps = jnp.transpose(long_taps, (1, 0, 2))
    gain = norm_gain.reshape(1, width)
    filt = medium_filter
    ext = (ROWS + 8, LANES)
    halo = (HALO, LANES)
    full = (ROWS, LANES)
    rows = (MODES, LANES)
    plane = (ROWS, width)
    modes = (MODES, width)

    mine = jnp.pad(jnp.concatenate([long_log_decay, long_residue], 1), ((0, 0), (0, LANES - 2 * MODES)))
    packed = swap(jnp.broadcast_to(mine[None], (count,) + mine.shape), "ctx")

    (tail,) = run(
        tail_kernel, "tail", width,
        [(med, "lane"), (lng, "lane"), (mtaps, "lane")],
        [((HALO, width), BF16, "lane")], [ext, rows],
    )
    before = passed_along(tail, "ctx", 1)

    rate, weight, q_two, k_two, gconv, z_all = run(
        long_kernel, "long", width,
        [(packed, "source"), (before, "lane"), (lng, "lane"), (ltaps, "lane"), (cotangent, "lane")],
        [(modes, F32, "lane"), (modes, F32, "lane"), (plane, BF16, "lane"), (plane, BF16, "lane"), (plane, BF16, "lane"), ((count,) + modes, BF16, "lane")],
        [ext, halo, full, rows],
    )
    zg = swap(z_all, "ctx")

    prod, q_one, k_one, v_one, conv, gated, square, y_back = run(
        medium_kernel, "medium", width,
        [(med, "lane"), (before, "lane"), (mtaps, "lane"), (filt, "lane"), (forward, "whole"), (top, "whole"), (gconv, "lane"), (rate, "lane"), (weight, "lane")],
        [((ROWS + TAPS, width), BF16, "lane"), (plane, BF16, "lane"), (plane, BF16, "lane"), (plane, BF16, "lane"), (plane, F32, "lane"), (plane, F32, "lane"), ((8, ROWS), F32, "whole"), (plane, F32, "lane")],
        [ext, halo, full],
    )
    grad_prod, zin, inner = run(
        inner_kernel, "inner", width,
        [(me, "scalar"), (zg, "lane"), (rate, "lane"), (weight, "lane"), (y_back, "lane"), (k_two, "lane"), (gated, "lane"), (gain, "lane")],
        [(plane, BF16, "lane"), (modes, F32, "lane"), ((8, ROWS), F32, "whole")],
        [full],
    )
    sums = swap(jnp.concatenate([square, inner], 1), "tp")

    x, gco, gq1, gk2, gain_row, edge = run(
        norm_kernel, "norm", width,
        [(sums, "whole"), (gated, "lane"), (conv, "lane"), (q_one, "lane"), (k_one, "lane"), (v_one, "lane"), (k_two, "lane"), (grad_prod, "lane"), (gain, "lane"), (filt, "lane"), (cotangent, "lane")],
        [(plane, BF16, "lane"), (plane, BF16, "lane"), (plane, F32, "lane"), (plane, F32, "lane"), ((8, width), F32, "lane"), ((HALO, width), BF16, "lane")],
        [full, rows],
    )
    after = passed_along(edge, "ctx", -1)
    (sent,) = run(
        filter_kernel, "filter", width,
        [(x, "lane"), (gco, "lane"), (gq1, "lane"), (gk2, "lane"), (gain_row, "lane"), (prod, "lane"), (med, "lane"), (lng, "lane"), (before, "lane"), (rate, "lane"), (forward, "whole"), (low, "whole")],
        [((count, MODES + 8, width), BF16, "lane")],
        [ext, halo, (SHARE * count + 8, LANES), full, (MODES + 8, LANES)],
    )
    got = swap(sent, "ctx")

    (ends,) = run(
        behind_kernel, "behind", width, [(gconv, "lane"), (rate, "lane")],
        [((2 * MODES, CHUNKS, width), F32, "lane")], [full],
    )
    y_front, mode_sums = run(
        modes_kernel, "modes", width,
        [(x, "lane"), (gconv, "lane"), (rate, "lane"), (weight, "lane"), (ends, "lane")],
        [(plane, F32, "lane"), ((5 * MODES, width), F32, "lane")],
        [full, full],
    )
    mixed, gq2, gk1, gv1, res, taps, nxt = run(
        answer_kernel, "answer", width,
        [(me, "scalar"), (got, "lane"), (rate, "lane"), (weight, "lane"), (y_front, "lane"), (q_two, "lane"), (cotangent, "lane"), (mode_sums, "lane"), (zin, "lane"), (after, "lane"), (gco, "lane"), (filt, "lane"), (k_one, "lane"), (v_one, "lane"), (med, "lane"), (lng, "lane"), (before, "lane"), (forward, "whole"), (low, "whole")],
        [(plane, BF16, "lane"), (plane, F32, "lane"), (plane, F32, "lane"), (plane, F32, "lane"), ((2 * MODES, width), F32, "lane"), ((MODES, width), F32, "lane"), ((8, width), F32, "lane")],
        [ext, halo, full, rows],
    )
    reduced = jnp.sum(got[:, MODES : MODES + SHARE].astype(F32), 0).astype(BF16)
    every = jnp.concatenate([reduced, taps[:9].astype(BF16)], 0)
    own = res.astype(BF16).reshape(2 * MODES, count, MODES).transpose(1, 0, 2).reshape(count, 1, width)
    last = swap(jnp.concatenate([jnp.broadcast_to(every[None], (count,) + every.shape), own], 1), "ctx")

    grad_med, grad_lng = run(
        input_kernel, "inputs", width,
        [(gq1, "lane"), (gk1, "lane"), (gv1, "lane"), (gq2, "lane"), (gk2, "lane"), (after, "lane"), (nxt, "lane"), (mtaps, "lane"), (ltaps, "lane")],
        [((3, ROWS, width), BF16, "lane"), ((2, ROWS, width), BF16, "lane")],
        [ext, rows],
    )
    taps_medium, taps_long, grad_filter, gain_total, grad_residue, grad_log = run(
        finish_kernel, "finish", width, [(last, "lane")],
        [((3, 3, width), F32, "lane"), ((3, 2, width), F32, "lane"), ((TAPS, width), F32, "lane"), ((1, width), F32, "lane"), ((MODES, MODES), F32, "whole"), ((MODES, MODES), F32, "whole")],
        [(SHARE * count + 8, LANES)],
    )
    return (
        mixed,
        jnp.transpose(grad_med, (1, 0, 2)),
        jnp.transpose(grad_lng, (1, 0, 2)),
        taps_medium,
        taps_long,
        grad_filter,
        gain_total.reshape(width),
        grad_residue,
        grad_log,
    )


def solution(mesh):
    return jax.shard_map(
        on_device,
        mesh=mesh,
        in_specs=(
            P("ctx", None, "tp"),
            P("ctx", None, "tp"),
            P(None, None, "tp"),
            P(None, None, "tp"),
            P(None, "tp"),
            P("tp"),
            P(("tp", "ctx"), None),
            P(("tp", "ctx"), None),
            P("ctx", "tp"),
        ),
        out_specs=(
            P("ctx", "tp"),
            P("ctx", None, "tp"),
            P("ctx", None, "tp"),
            P(None, None, "tp"),
            P(None, None, "tp"),
            P(None, "tp"),
            P("tp"),
            P(("tp", "ctx"), None),
            P(("tp", "ctx"), None),
        ),
        check_vma=False,
    )
```

```python
import functools
import math

import jax
import jax.numpy as jnp
import ml_dtypes
import numpy as np
from jax import lax
from jax.experimental import pallas as pl
from jax.experimental.pallas import tpu as pltpu
from jax.sharding import PartitionSpec as P

D = 4096
MODES = 16
TAPS = 128
ROWS = 256
LANES = 128
CHUNKS = 8
STEPS = ROWS // CHUNKS
HALO = 144
WIDE = ROWS + TAPS
Q_END = TAPS
LONG_END = TAPS + 6
SHARE = 5
PAIRS = 16
HALF = SHARE * PAIRS
F32 = jnp.float32
BF16 = jnp.bfloat16
precise = lax.Precision.HIGHEST


def fourier_matrices():
    size = 2 * TAPS
    place = np.arange(size)
    mode = np.arange(TAPS)
    turn = 2.0 * math.pi / size
    cos_part = np.cos(turn * ((mode[:, None] * place[None, :]) % size))
    sin_part = -np.sin(turn * ((mode[:, None] * place[None, :]) % size))
    sin_part[0] = 1.0 - 2.0 * (place % 2)
    forward = np.concatenate([cos_part, sin_part], 0)
    weight = np.full((size,), 2.0 / size)
    weight[0] = weight[TAPS] = 1.0 / size
    backward = (forward * weight[:, None]).T

    return tuple(
        table.astype(ml_dtypes.bfloat16) for table in (forward, backward[:TAPS], backward[TAPS:])
    )


def f32_of(value):
    return value.astype(F32)


def rounded(value):
    return value.astype(BF16).astype(F32)


def spectrum(table, signal):
    return jnp.dot(table, signal, preferred_element_type=F32)


def from_spectrum(table, values):
    return jnp.dot(table, values.astype(BF16), preferred_element_type=F32)


def split_spectrum(values):
    real, imag = values[:TAPS], values[TAPS:]
    first = lax.broadcasted_iota(jnp.int32, real.shape, 0) == 0
    return real, jnp.where(first, imag, real), jnp.where(first, 0.0, imag)


def spread(value, row):
    return jnp.broadcast_to(value[row : row + 1, :], (CHUNKS, LANES))


def chunk_index():
    return lax.broadcasted_iota(jnp.int32, (CHUNKS, LANES), 0)


def at_step(ref, step):
    return ref[pl.ds(step, CHUNKS, stride=STEPS), :]


def chunk_states(source, rate, backward):
    decay = jnp.exp(-rate)
    decays = [spread(decay, r) for r in range(MODES)]

    def body(n, states):
        value = at_step(source, STEPS - 1 - n if backward else n)
        return tuple(decays[r] * states[r] + value for r in range(MODES))

    first = at_step(source, 0)
    return lax.fori_loop(0, STEPS, body, (first - first,) * MODES, unroll=4)


def powers(rate):
    return [jnp.exp(rate * float(-STEPS * by)) for by in (1, 2, 4)]


def chunk_entries(ends, power, backward):
    place = chunk_index()
    inside = [place < CHUNKS - by if backward else place >= by for by in (1, 2, 4)]
    entries = []
    for r in range(MODES):
        total = ends[r]
        for level, by in enumerate((1, 2, 4)):
            moved = pltpu.roll(total, CHUNKS - by if backward else by, 0)
            total = total + jnp.where(inside[level], spread(power[level], r) * moved, 0.0)
        moved = pltpu.roll(total, CHUNKS - 1 if backward else 1, 0)
        entries.append(jnp.where(inside[0], moved, 0.0))
    return entries


def chunk_weights(power, backward):
    after = chunk_index() if backward else CHUNKS - 1 - chunk_index()
    bits = [(after & by) != 0 for by in (1, 2, 4)]

    def weight(r):
        parts = [jnp.where(bit, spread(level, r), 1.0) for bit, level in zip(bits, power)]
        return parts[0] * parts[1] * parts[2]

    return weight, after.astype(F32) * float(STEPS)


def local_answer(source, target, rate, weight, entries, backward):
    decay = jnp.exp(-rate)
    decays = [spread(decay, r) for r in range(MODES)]
    weights = [spread(weight, r) for r in range(MODES)]

    def body(n, states):
        step = STEPS - 1 - n if backward else n
        value = at_step(source, step)
        states = tuple(decays[r] * states[r] + value for r in range(MODES))
        terms = [weights[r] * states[r] for r in range(MODES)]
        while len(terms) > 1:
            terms = [terms[k] + terms[k + 1] for k in range(0, len(terms), 2)]
        target[pl.ds(step, CHUNKS, stride=STEPS), :] = terms[0]
        return states

    lax.fori_loop(0, STEPS, body, tuple(entries), unroll=2)


def add_entry(local, target, rate, weight, entry, backward, inside=None):
    decay = jnp.exp(-rate)
    decays = [spread(decay, r) for r in range(MODES)]
    start = weight * entry
    factor, _ = chunk_weights(powers(rate), not backward)
    parts = [spread(start, r) * factor(r) for r in range(MODES)]
    if inside is not None:
        parts = [parts[r] + spread(weight, r) * inside[r] for r in range(MODES)]

    def body(n, parts):
        step = STEPS - 1 - n if backward else n
        parts = tuple(decays[r] * parts[r] for r in range(MODES))
        terms = list(parts)
        while len(terms) > 1:
            terms = [terms[k] + terms[k + 1] for k in range(0, len(terms), 2)]
        target[pl.ds(step, CHUNKS, stride=STEPS), :] = at_step(local, step) + terms[0]
        return parts

    lax.fori_loop(0, STEPS, body, tuple(parts), unroll=4)


def pair_state(early, late, rate, backward):
    near = jnp.exp(rate * float(-ROWS))
    return early + near * late if backward else near * early + late


def entry_state(gathered, other, rate, me, backward):
    far = jnp.exp(rate * float(-2 * ROWS))
    near = jnp.exp(rate * float(-ROWS))
    pair, second = me // 2, me % 2
    pairs = gathered.shape[0]

    def body(n, state):
        index = pairs - 1 - n if backward else n
        return far * state + gathered[index, 0:MODES, :].astype(F32)

    count = pairs - 1 - pair if backward else pair
    state = lax.fori_loop(0, count, body, jnp.zeros((MODES, LANES), F32))
    outer = second if backward else 1 - second
    return jnp.where(outer == 1, state, near * state + other)


def extend(ext, before, body):
    ext[6:8, :] = before
    ext[8 : 8 + ROWS, :] = body


def three(ext, taps):
    return (
        taps[0:1] * ext[8 : 8 + ROWS, :]
        + taps[1:2] * ext[7 : 7 + ROWS, :]
        + taps[2:3] * ext[6 : 6 + ROWS, :]
    )


def store_tap_sums(target, row, grad, ext):
    for shift in range(3):
        target[row + shift : row + shift + 1, :] = jnp.sum(
            grad * ext[8 - shift : 8 - shift + ROWS, :], 0, keepdims=True
        )


def tail_kernel(med, ends, taps, out, ext, rows):
    feats = []
    for j in (1, 2):
        extend(ext, jnp.zeros((2, LANES), F32), f32_of(med[j]))
        feats.append(rounded(three(ext, taps[j])))
    out[0:TAPS, :] = (feats[0][TAPS:] * feats[1][TAPS:]).astype(BF16)
    rows[...] = jnp.zeros(rows.shape, F32)
    for j in range(3):
        ext[8 : 8 + ROWS, :] = f32_of(med[j])
        rows[2 * j : 2 * j + 2, :] = ext[6 + ROWS : 8 + ROWS, :]
    rows[6:10, :] = ends[...]
    out[TAPS:HALO, :] = rows[...].astype(BF16)


def long_kernel(packed, before, lng, taps, cot, rate_out, weight_out, q_out, k_out, g_out, z_out, ends_out, ext, halo, grad, rows):
    both = jnp.transpose(packed[...].reshape(LANES, LANES))
    rate = jnp.exp(both[:MODES])
    rate_out[...] = rate
    weight_out[...] = both[MODES : 2 * MODES] * jnp.sqrt(2.0 * rate)
    halo[...] = f32_of(before[...])
    feats = []
    for j in range(2):
        extend(ext, halo[LONG_END + 2 * j : LONG_END + 2 * j + 2, :], f32_of(lng[j]))
        feats.append(three(ext, taps[j]).astype(BF16))
    q_out[...] = feats[0]
    k_out[...] = feats[1]
    sent = (f32_of(cot[...]) * f32_of(feats[0])).astype(BF16)
    g_out[...] = sent
    grad[...] = f32_of(sent)
    states = chunk_states(grad, rate, True)
    factor, _ = chunk_weights(powers(rate), True)
    for r in range(MODES):
        ends_out[r] = states[r]
        rows[r : r + 1, :] = jnp.sum(factor(r) * states[r], 0, keepdims=True)
    z_out[...] = rows[...].astype(BF16)


def join_kernel(me, own, other, rate, slot_out):
    first = me[0] % 2 == 0
    mine, theirs = f32_of(own[...]), f32_of(other[...])
    early, late = jnp.where(first, mine, theirs), jnp.where(first, theirs, mine)
    joined = pair_state(early, late, rate[...], True).astype(BF16)
    slot_out[...] = jnp.broadcast_to(joined[None], slot_out.shape)


def medium_kernel(med, before, taps, filt, forward, top,
                  prod_out, q_out, k_out, v_out, conv_out, gated_out, sq_out, ext, halo):
    halo[...] = f32_of(before[...])
    feats = []
    for j in range(3):
        extend(ext, halo[TAPS + 2 * j : TAPS + 2 * j + 2, :], f32_of(med[j]))
        feats.append(three(ext, taps[j]).astype(BF16))
    query, key, value = feats
    q_out[...] = query
    k_out[...] = key
    v_out[...] = value
    prod_out[0:TAPS, :] = before[0:TAPS, :]
    prod_out[TAPS:, :] = (f32_of(key) * f32_of(value)).astype(BF16)
    windows = jnp.concatenate([prod_out[0 : 2 * TAPS, :], prod_out[TAPS:, :]], 1)
    win = spectrum(forward[...], windows)
    ker = spectrum(forward[:, 0:TAPS], filt[...])
    ker_re, ker_alt, ker_im = split_spectrum(ker)
    ker_re, ker_alt, ker_im = (jnp.concatenate([k, k], 1) for k in (ker_re, ker_alt, ker_im))
    re, im = win[:TAPS], win[TAPS:]
    spec = jnp.concatenate([re * ker_re - im * ker_im, im * ker_alt + re * ker_im], 0)
    answer = from_spectrum(top[...], spec)
    conv = jnp.concatenate([answer[:, :LANES], answer[:, LANES:]], 0)
    conv_out[...] = conv
    gated = f32_of(query) * conv
    gated_out[...] = gated
    part = lax.dot_general(
        jnp.ones((8, LANES), F32), gated * gated, (((1,), (1,)), ((), ())),
        precision=precise, preferred_element_type=F32,
    )

    @pl.when(pl.program_id(0) == 0)
    def _():
        sq_out[...] = jnp.zeros(sq_out.shape, F32)

    sq_out[...] += part


def back_kernel(gconv, rate, weight, ends, y_out, grad):
    grad[...] = f32_of(gconv[...])
    entries = chunk_entries([ends[r] for r in range(MODES)], powers(rate[...]), True)
    local_answer(grad, y_out, rate[...], weight[...], entries, True)


def inner_kernel(me, zg, z_other, rate, weight, y_loc, k_two, gated, gain, square, gp_out, zin_out, in_out, full, total):
    entry = entry_state(zg, f32_of(z_other[...]), rate[...], me[0], True)
    zin_out[...] = entry
    add_entry(y_loc, full, rate[...], weight[...], entry, True)
    sent = full[...].astype(BF16)
    gp_out[...] = sent
    product = f32_of(sent) * f32_of(k_two[...]) * gain[...] * gated[...]
    part = lax.dot_general(
        jnp.ones((8, LANES), F32), product, (((1,), (1,)), ((), ())),
        precision=precise, preferred_element_type=F32,
    )

    @pl.when(pl.program_id(0) == 0)
    def _():
        total[...] = part

    @pl.when(pl.program_id(0) > 0)
    def _():
        total[...] += part

    @pl.when(pl.program_id(0) == pl.num_programs(0) - 1)
    def _():
        for device in range(in_out.shape[0]):
            in_out[device, 0:1, 0:ROWS] = square[0:1, :]
            in_out[device, 0:1, ROWS:] = total[0:1, :]


def norm_kernel(me, sums, gated, conv, q_one, k_one, v_one, k_two, gp, gain, filt, cot, prod, med, lng, before, rate, forward, low,
                x_out, gco_out, gq1_out, gk2_out, e_out, pair_out, keep_out, work, tail, ext, halo, f_out):
    ones = jnp.ones((8, LANES), F32)

    def column(values):
        return lax.dot_general(
            values, ones, (((0,), (0,)), ((), ())), precision=precise, preferred_element_type=F32
        )

    square = column(sums[:, 0, 0:ROWS]) / float(D) + 1e-06
    inner = column(sums[:, 0, ROWS:]) / float(D)
    scale = lax.rsqrt(square)
    gate = gated[...]
    key_two = f32_of(k_two[...])
    normed = rounded(gate * scale * gain[...])
    prod_two = (key_two * normed).astype(BF16)
    x_out[...] = prod_two
    grad_two = f32_of(gp[...])
    grad_k_two = grad_two * normed
    gk2_out[...] = grad_k_two
    grad_normed = grad_two * key_two
    f_out[TAPS:, :] = jnp.zeros((f_out.shape[0] - TAPS, LANES), F32)
    f_out[TAPS : TAPS + 1, :] = jnp.sum(grad_normed * gate * scale, 0, keepdims=True)
    grad_gated = scale * (grad_normed * gain[...] - gate * scale * scale * inner)
    grad_q_one = grad_gated * conv[...]
    gq1_out[...] = grad_q_one
    gco = (grad_gated * f32_of(q_one[...])).astype(BF16)
    gco_out[...] = gco
    e_out[0:TAPS, :] = gco[0:TAPS]
    tail[...] = jnp.zeros(tail.shape, F32)
    tail[0:2, :] = grad_q_one[0:2]
    work[...] = f32_of(gco)
    taps = f32_of(filt[...])
    for shift in range(2):
        head = jnp.sum(taps * work[shift : shift + TAPS, :], 0, keepdims=True)
        tail[2 + shift : 3 + shift, :] = head * f32_of(v_one[0:16, :])[shift : shift + 1]
        tail[4 + shift : 5 + shift, :] = head * f32_of(k_one[0:16, :])[shift : shift + 1]
    tail[6:8, :] = grad_k_two[0:2]
    tail[8:10, :] = f32_of(prod_two)[0:2]
    tail[10:12, :] = f32_of(cot[0:16, :])[0:2]
    e_out[TAPS:HALO, :] = tail[...].astype(BF16)
    halo[...] = f32_of(before[...])
    extend(ext, halo[Q_END : Q_END + 2, :], f32_of(med[0]))
    store_tap_sums(f_out, TAPS + 1, grad_q_one, ext)
    extend(ext, halo[LONG_END + 2 : LONG_END + 4, :], f32_of(lng[1]))
    store_tap_sums(f_out, TAPS + 4, grad_k_two, ext)
    win = spectrum(forward[...], jnp.concatenate([prod[0 : 2 * TAPS, :], prod[TAPS:, :]], 1))
    grd = spectrum(forward[:, TAPS:], jnp.concatenate([gco[0:TAPS], gco[TAPS:]], 1))
    win_re, win_alt, win_im = split_spectrum(win)
    re, im = grd[:TAPS], grd[TAPS:]
    spec = jnp.concatenate([re * win_re + im * win_im, im * win_alt - re * win_im], 0)
    f_out[0:TAPS, :] = from_spectrum(low[...], spec[:, :LANES] + spec[:, LANES:])
    work[...] = f32_of(prod_two)
    states = chunk_states(work, rate[...], False)
    factor, _ = chunk_weights(powers(rate[...]), False)
    for r in range(MODES):
        tail[r : r + 1, :] = jnp.sum(factor(r) * states[r], 0, keepdims=True)
    second = me[0] % 2
    pair_out[0:MODES, :] = tail[...].astype(BF16)
    pair_out[MODES:, :] = f_out[pl.ds(pl.multiple_of(HALF * (1 - second), 16), HALF), :].astype(BF16)
    keep_out[...] = f_out[pl.ds(pl.multiple_of(HALF * second, 16), HALF), :]


def share_kernel(me, pair, got, keep, rate, slot_out, add, slot):
    first = me[0] % 2 == 0
    mine, theirs = f32_of(pair[0:MODES, :]), f32_of(got[0:MODES, :])
    early, late = jnp.where(first, mine, theirs), jnp.where(first, theirs, mine)
    slot[0:MODES, :] = pair_state(early, late, rate[...], False)
    add[HALF:, :] = jnp.zeros((8, add.shape[1]), F32)
    add[0:HALF, :] = keep[...] + f32_of(got[MODES:, :])
    for device in range(slot_out.shape[0]):
        slot[MODES:, :] = add[SHARE * device : SHARE * device + 8, :]
        slot_out[device] = slot[...].astype(BF16)


def behind_kernel(g, rate, ends_out, gs):
    gs[...] = f32_of(g[...])
    decay = jnp.exp(-rate[...])
    first = at_step(gs, 0)
    zero = first - first
    half = MODES // 2
    for base in range(0, MODES, half):
        decays = [spread(decay, base + r) for r in range(half)]

        def behind(n, carry):
            z, q = carry
            grad = at_step(gs, STEPS - 1 - n)
            q = tuple(decays[r] * (q[r] + z[r]) for r in range(half))
            z = tuple(decays[r] * z[r] + grad for r in range(half))
            return z, q

        z, q = lax.fori_loop(0, STEPS, behind, ((zero,) * half,) * 2, unroll=4)
        for r in range(half):
            ends_out[base + r] = z[r]
            ends_out[MODES + base + r] = q[r]


def modes_kernel(x, g, rate, weight, ends, y_out, sums_out, entry_out, xs, gs):
    xs[...] = f32_of(x[...])
    gs[...] = f32_of(g[...])
    rates = rate[...]
    decay = jnp.exp(-rates)
    first = at_step(xs, 0)
    zero = first - first
    half = MODES // 2
    power = powers(rates)
    s_end, q_end, plain, slope = [], [], [], []
    z_end = [ends[r] for r in range(MODES)]
    zq_end = [ends[MODES + r] for r in range(MODES)]
    for base in range(0, MODES, half):
        decays = [spread(decay, base + r) for r in range(half)]
        weights = [spread(weight, base + r) for r in range(half)]

        def ahead(n, carry):
            s, q, p, l = carry
            value, grad = at_step(xs, n), at_step(gs, n)
            q = tuple(decays[r] * (q[r] + s[r]) for r in range(half))
            s = tuple(decays[r] * s[r] + value for r in range(half))
            p = tuple(p[r] + grad * s[r] for r in range(half))
            l = tuple(l[r] + grad * q[r] for r in range(half))
            terms = [weights[r] * s[r] for r in range(half)]
            while len(terms) > 1:
                terms = [terms[k] + terms[k + 1] for k in range(0, len(terms), 2)]
            answer = terms[0] if base == 0 else at_step(y_out, n) + terms[0]
            y_out[pl.ds(n, CHUNKS, stride=STEPS), :] = answer
            return s, q, p, l

        s, q, p, l = lax.fori_loop(0, STEPS, ahead, ((zero,) * half,) * 4, unroll=4)
        s_end += s
        q_end += q
        plain += p
        slope += l
    entries = chunk_entries(s_end, power, False)
    exits = chunk_entries(z_end, power, True)
    back, back_steps = chunk_weights(power, True)
    front, front_steps = chunk_weights(power, False)
    for r in range(MODES):
        a = spread(decay, r)
        a_step = a * spread(power[0], r)
        one = plain[r] + entries[r] * a * z_end[r]
        two = (
            slope[r]
            + float(STEPS) * a_step * entries[r] * exits[r]
            + a * (entries[r] * zq_end[r] + exits[r] * (q_end[r] + s_end[r]))
        )
        back_r, front_r = back(r), front(r)
        rows = (
            one,
            two,
            back_r * z_end[r],
            back_r * (zq_end[r] + back_steps * z_end[r]),
            front_r * (q_end[r] + s_end[r] + front_steps * s_end[r]),
        )
        for kind, value in enumerate(rows):
            place = kind * MODES + r
            sums_out[place : place + 1, :] = jnp.sum(value, 0, keepdims=True)
    for r in range(MODES):
        entry_out[r] = entries[r]


def kernel_spectrum(forward, filt, copies):
    parts = split_spectrum(spectrum(forward[:, 0:TAPS], filt[...]))
    return [jnp.concatenate([part] * copies, 1) if copies > 1 else part for part in parts]


def local_taps(gco, filt, k_one, v_one, med, before, forward, low, grad_out, taps_out, ext, halo):
    second = gco[TAPS:, :]
    pieces = jnp.concatenate(
        [gco[...], jnp.concatenate([second, jnp.zeros(second.shape, BF16)], 0)], 1
    )
    win = spectrum(forward[...], pieces)
    ker_re, ker_alt, ker_im = kernel_spectrum(forward, filt, 2)
    re, im = win[:TAPS], win[TAPS:]
    spec = jnp.concatenate([re * ker_re + im * ker_im, im * ker_alt - re * ker_im], 0)
    answer = from_spectrum(low[...], spec)
    grad_prod = jnp.concatenate([answer[:, :LANES], answer[:, LANES:]], 0)
    grad_out[...] = grad_prod
    halo[...] = f32_of(before[...])
    taps_out[...] = jnp.zeros(taps_out.shape, F32)
    for place, other in enumerate((v_one, k_one)):
        extend(ext, halo[TAPS + 2 + 2 * place : TAPS + 4 + 2 * place, :], f32_of(med[place + 1]))
        store_tap_sums(taps_out, 3 * place, grad_prod * f32_of(other[...]), ext)


def answer_kernel(me, sg, pair, other, rate, weight, y_loc, inside, q_two, cot, sums, zin, lng, before, tap_rows, after, filt, k_one, v_one, med, forward, low,
                  mixed_out, gq2_out, res_out, row_out, exit_out, late_out, ext, halo, full, rows):
    rates = rate[...]
    entry = entry_state(sg, f32_of(other[0:MODES, :]), rates, me[0], False)
    add_entry(y_loc, full, rates, weight[...], entry, False, inside)
    conv = rounded(full[...])
    grad_out = f32_of(cot[...])
    mixed_out[...] = (f32_of(q_two[...]) * conv).astype(BF16)
    grad_q_two = grad_out * conv
    gq2_out[...] = grad_q_two
    decay = jnp.exp(-rates)
    exit_out[...] = jnp.exp(rates * float(-ROWS)) * entry + f32_of(pair[0:MODES, :])
    plain = sums[0:MODES, :] + entry * decay * sums[2 * MODES : 3 * MODES, :]
    slope = (
        sums[MODES : 2 * MODES, :]
        + float(ROWS) * jnp.exp(rates * float(-ROWS - 1)) * entry * zin[...]
        + decay * (entry * sums[3 * MODES : 4 * MODES, :] + zin[...] * sums[4 * MODES :, :])
    )
    res_out[0:MODES, :] = (jnp.sqrt(2.0 * rates) * plain).astype(BF16)
    res_out[MODES:, :] = (weight[...] * (0.5 * plain - rates * slope)).astype(BF16)
    added = f32_of(sg[0])
    for device in range(1, sg.shape[0]):
        added = added + f32_of(sg[device])
    rows[0:8, :] = added[MODES : MODES + 8]
    rows[SHARE : SHARE + 6, :] = tap_rows[0:6, :]
    win = spectrum(forward[:, TAPS:], after[0:TAPS, :])
    ker_re, ker_alt, ker_im = kernel_spectrum(forward, filt, 1)
    re, im = win[:TAPS], win[TAPS:]
    spec = jnp.concatenate([re * ker_re + im * ker_im, im * ker_alt - re * ker_im], 0)
    late = from_spectrum(low[...], spec)
    late_out[...] = late
    for place, other in enumerate((v_one, k_one)):
        ext[0:ROWS, :] = f32_of(med[place + 1])
        grad = late * f32_of(other[TAPS:, :])
        for shift in range(3):
            row = SHARE + 3 * place + shift
            rows[row : row + 1, :] += jnp.sum(grad * ext[TAPS - shift : ROWS - shift, :], 0, keepdims=True)
    halo[...] = f32_of(before[TAPS:HALO, :])
    extend(ext, halo[6:8, :], f32_of(lng[0]))
    store_tap_sums(rows, SHARE + 6, grad_q_two, ext)
    row_out[...] = rows[...].astype(BF16)


def input_kernel(gq1, gpo, late, gq2, gk2, k_one, v_one, after, leave, rate, weight, mtaps, ltaps,
                 med_out, lng_out, ext, tail, nxt):
    tail[...] = f32_of(after[TAPS:HALO, :])
    grad_prod = jnp.concatenate([gpo[0:TAPS, :], gpo[TAPS:, :] + late[...]], 0)
    state = leave[...]
    decay = jnp.exp(-rate[...])
    for step in range(2):
        state = decay * state + tail[8 + step : 9 + step, :]
        value = rounded(jnp.sum(weight[...] * state, 0, keepdims=True))
        nxt[step : step + 1, :] = value * tail[10 + step : 11 + step, :]

    def back(grad, following, taps):
        ext[0:ROWS, :] = grad
        ext[ROWS : ROWS + 2, :] = following
        return (
            taps[0:1] * ext[0:ROWS, :] + taps[1:2] * ext[1 : ROWS + 1, :] + taps[2:3] * ext[2 : ROWS + 2, :]
        ).astype(BF16)

    med_out[0] = back(gq1[...], tail[0:2, :], mtaps[0])
    med_out[1] = back(grad_prod * f32_of(v_one[...]), tail[2:4, :], mtaps[1])
    med_out[2] = back(grad_prod * f32_of(k_one[...]), tail[4:6, :], mtaps[2])
    lng_out[0] = back(gq2[...], nxt[0:2, :], ltaps[0])
    lng_out[1] = back(gk2[...], tail[6:8, :], ltaps[1])


def finish_kernel(last, mtap_out, ltap_out, filt_out, gain_out, res_out, log_out, f_all):
    added = jnp.zeros((last.shape[1], LANES), F32)
    for place in range(last.shape[0]):
        second, pair = place // PAIRS, place % PAIRS
        piece = f32_of(last[2 * pair + second])
        f_all[SHARE * place : SHARE * place + 8, :] = piece[0:8]
        added = added + piece
    filt_out[...] = f_all[0:TAPS, :]
    gain_out[...] = f_all[TAPS : TAPS + 1, :]
    for shift in range(3):
        mtap_out[shift, 0:1, :] = f_all[TAPS + 1 + shift : TAPS + 2 + shift, :]
        ltap_out[shift, 1:2, :] = f_all[TAPS + 4 + shift : TAPS + 5 + shift, :]
        mtap_out[shift, 1:2, :] = added[SHARE + shift : SHARE + 1 + shift]
        mtap_out[shift, 2:3, :] = added[SHARE + 3 + shift : SHARE + 4 + shift]
        ltap_out[shift, 0:1, :] = added[SHARE + 6 + shift : SHARE + 7 + shift]
    block = pl.program_id(0)
    lane = lax.broadcasted_iota(jnp.int32, (MODES, LANES), 1)
    row = lax.broadcasted_iota(jnp.int32, (MODES, LANES), 0)
    picked = jnp.where(lane % MODES == row, added[SHARE + 9 : SHARE + 10], 0.0)
    goal = (row == lane // MODES + 8 * (block % 2)).astype(F32)
    part = lax.dot_general(
        picked, goal, (((1,), (1,)), ((), ())), precision=precise, preferred_element_type=F32
    )

    @pl.when(block == 0)
    def _():
        res_out[...] = part

    @pl.when(block == 1)
    def _():
        res_out[...] += part

    @pl.when(block == 2)
    def _():
        log_out[...] = part

    @pl.when(block == 3)
    def _():
        log_out[...] += part


def block_of(shape, kind, lanes):
    if kind == "lane":
        lead = shape[:-1]
        return pl.BlockSpec(lead + (lanes,), lambda l: (0,) * len(lead) + (l,))
    if kind == "whole":
        return pl.BlockSpec(shape, lambda l: (0,) * len(shape))
    if kind == "source":
        return pl.BlockSpec((8,) + shape[1:], lambda l: (l,) + (0,) * (len(shape) - 1))
    return pl.BlockSpec(memory_space=pltpu.SMEM)


def run(kernel, name, width, inputs, outputs, scratch, limit=63, flops=1000000, lanes=LANES):
    arrays = [array for array, _ in inputs]
    moved = sum(a.size * a.dtype.itemsize for a in arrays)
    return pl.pallas_call(
        kernel,
        grid=(width // lanes,),
        in_specs=[block_of(a.shape, kind, lanes) for a, kind in inputs],
        out_specs=[block_of(shape, kind, lanes) for shape, _, kind in outputs],
        out_shape=[
            jax.ShapeDtypeStruct(shape, dtype) for shape, dtype, _ in outputs
        ],
        scratch_shapes=[pltpu.VMEM(shape, F32) for shape in scratch],
        compiler_params=pltpu.CompilerParams(vmem_limit_bytes=limit * 1024 * 1024),
        cost_estimate=pl.CostEstimate(flops=flops, bytes_accessed=moved, transcendentals=0),
        name=name,
    )(*arrays)


def passed_along(array, axis, by):
    count = lax.axis_size(axis)
    pairs = [(i, i + by) for i in range(count) if 0 <= i + by < count]
    return lax.ppermute(array, axis, pairs)


def exchanged(array):
    return lax.ppermute(array, "ctx", [(i, i ^ 1) for i in range(lax.axis_size("ctx"))])


def in_plane(array):
    groups = [[2 * p + z for p in range(PAIRS)] for z in range(2)]
    return lax.all_to_all(array, "ctx", split_axis=0, concat_axis=0, tiled=True, axis_index_groups=groups)


def swap(array, axis):
    return lax.all_to_all(array, axis, split_axis=0, concat_axis=0, tiled=True)


def on_device(medium_input, long_input, medium_taps, long_taps, medium_filter, norm_gain, long_residue, long_log_decay, cotangent):
    width = cotangent.shape[1]
    count = lax.axis_size("ctx")
    me = lax.axis_index("ctx").astype(jnp.int32).reshape(1)
    forward, low, top = (jnp.asarray(table) for table in fourier_matrices())
    med = jnp.transpose(medium_input, (1, 0, 2))
    lng = jnp.transpose(long_input, (1, 0, 2))
    mtaps = jnp.transpose(medium_taps, (1, 0, 2))
    ltaps = jnp.transpose(long_taps, (1, 0, 2))
    gain = norm_gain.reshape(1, width)
    filt = medium_filter
    ext = (ROWS + 8, LANES)
    halo = (HALO, LANES)
    wide = (WIDE, width)
    full = (ROWS, LANES)
    rows = (MODES, LANES)
    plane = (ROWS, width)
    modes = (MODES, width)

    mine = jnp.pad(jnp.concatenate([long_log_decay, long_residue], 1), ((0, 0), (0, LANES - 2 * MODES)))
    packed = swap(jnp.broadcast_to(mine[None], (count,) + mine.shape), "ctx")

    ends = jnp.transpose(long_input[ROWS - 2 :].astype(F32), (1, 0, 2)).reshape(4, width)
    (tail,) = run(
        tail_kernel, "tail", width, [(med, "lane"), (ends, "lane"), (mtaps, "lane")],
        [((HALO, width), BF16, "lane")], [ext, rows], limit=16,
    )
    before = passed_along(tail, "ctx", 1)

    rate, weight, q_two, k_two, gconv, z_all, z_ends = run(
        long_kernel, "long", width,
        [(packed, "source"), (before, "lane"), (lng, "lane"), (ltaps, "lane"), (cotangent, "lane")],
        [(modes, F32, "lane"), (modes, F32, "lane"), (plane, BF16, "lane"), (plane, BF16, "lane"), (plane, BF16, "lane"), (modes, BF16, "lane"), ((MODES, CHUNKS, width), F32, "lane")],
        [ext, halo, full, rows],
    )
    z_other = exchanged(z_all)
    prod, q_one, k_one, v_one, conv, gated, square = run(
        medium_kernel, "medium", width,
        [(med, "lane"), (before, "lane"), (mtaps, "lane"), (filt, "lane"), (forward, "whole"), (top, "whole")],
        [(wide, BF16, "lane"), (plane, BF16, "lane"), (plane, BF16, "lane"), (plane, BF16, "lane"), (plane, F32, "lane"), (plane, F32, "lane"), ((8, ROWS), F32, "whole")],
        [ext, halo],
    )
    z_other, square = lax.optimization_barrier((z_other, square))
    (z_pairs,) = run(
        join_kernel, "join", width, [(me, "scalar"), (z_all, "lane"), (z_other, "lane"), (rate, "lane")],
        [((PAIRS,) + modes, BF16, "lane")], [], lanes=width,
    )
    zg = in_plane(z_pairs)
    (y_back,) = run(
        back_kernel, "back", width,
        [(gconv, "lane"), (rate, "lane"), (weight, "lane"), (z_ends, "lane")],
        [(plane, F32, "lane")], [full],
    )
    grad_prod, zin, inner = run(
        inner_kernel, "inner", width,
        [(me, "scalar"), (zg, "lane"), (z_other, "lane"), (rate, "lane"), (weight, "lane"), (y_back, "lane"), (k_two, "lane"), (gated, "lane"), (gain, "lane"), (square, "whole")],
        [(plane, BF16, "lane"), (modes, F32, "lane"), ((8, 1, 2 * ROWS), F32, "whole")],
        [full, (8, ROWS)],
    )
    sums = swap(inner, "tp")
    later, _ = lax.optimization_barrier((gconv, inner))
    (ends_back,) = run(
        behind_kernel, "behind", width, [(later, "lane"), (rate, "lane")],
        [((2 * MODES, CHUNKS, width), F32, "lane")], [full],
    )
    sums, ends_back = lax.optimization_barrier((sums, ends_back))

    x, gco, gq1, gk2, edge, pair, keep = run(
        norm_kernel, "norm", width,
        [(me, "scalar"), (sums, "whole"), (gated, "lane"), (conv, "lane"), (q_one, "lane"), (k_one, "lane"), (v_one, "lane"), (k_two, "lane"), (grad_prod, "lane"), (gain, "lane"), (filt, "lane"), (cotangent, "lane"), (prod, "lane"), (med, "lane"), (lng, "lane"), (before, "lane"), (rate, "lane"), (forward, "whole"), (low, "whole")],
        [(plane, BF16, "lane"), (plane, BF16, "lane"), (plane, F32, "lane"), (plane, F32, "lane"), ((HALO, width), BF16, "lane"), ((MODES + HALF, width), BF16, "lane"), ((HALF, width), F32, "lane")],
        [full, rows, ext, halo, (2 * HALF, LANES)],
    )
    after = passed_along(edge, "ctx", -1)
    other = exchanged(pair)
    gpo, tap_rows = run(
        local_taps, "taps", width,
        [(gco, "lane"), (filt, "lane"), (k_one, "lane"), (v_one, "lane"), (med, "lane"), (before, "lane"), (forward, "whole"), (low, "whole")],
        [(plane, F32, "lane"), ((8, width), F32, "lane")], [ext, halo],
    )
    other, after, tap_rows = lax.optimization_barrier((other, after, tap_rows))
    (sent,) = run(
        share_kernel, "share", width,
        [(me, "scalar"), (pair, "lane"), (other, "lane"), (keep, "lane"), (rate, "lane")],
        [((PAIRS, MODES + 8, width), BF16, "lane")], [(HALF + 8, width), (MODES + 8, width)], lanes=width,
    )
    got = in_plane(sent)

    y_front, mode_sums, inside = run(
        modes_kernel, "modes", width,
        [(x, "lane"), (gconv, "lane"), (rate, "lane"), (weight, "lane"), (ends_back, "lane")],
        [(plane, F32, "lane"), ((5 * MODES, width), F32, "lane"), ((MODES, CHUNKS, width), F32, "lane")], [full, full],
    )
    mixed, gq2, res, every, leave, late = run(
        answer_kernel, "answer", width,
        [(me, "scalar"), (got, "lane"), (pair, "lane"), (other, "lane"), (rate, "lane"), (weight, "lane"), (y_front, "lane"), (inside, "lane"), (q_two, "lane"), (cotangent, "lane"), (mode_sums, "lane"), (zin, "lane"), (lng, "lane"), (before, "lane"), (tap_rows, "lane"), (after, "lane"), (filt, "lane"), (k_one, "lane"), (v_one, "lane"), (med, "lane"), (forward, "whole"), (low, "whole")],
        [(plane, BF16, "lane"), (plane, F32, "lane"), ((2 * MODES, width), BF16, "lane"), ((MODES, width), BF16, "lane"), (modes, F32, "lane"), ((TAPS, width), F32, "lane")],
        [ext, rows, full, rows],
    )
    every = jnp.broadcast_to(every[None, : SHARE + 9], (count, SHARE + 9, width))
    own = res.reshape(2 * MODES, count, MODES).transpose(1, 0, 2).reshape(count, 1, width)
    last = swap(jnp.concatenate([every, own], 1), "ctx")

    grad_med, grad_lng = run(
        input_kernel, "inputs", width,
        [(gq1, "lane"), (gpo, "lane"), (late, "lane"), (gq2, "lane"), (gk2, "lane"), (k_one, "lane"), (v_one, "lane"), (after, "lane"), (leave, "lane"), (rate, "lane"), (weight, "lane"), (mtaps, "lane"), (ltaps, "lane")],
        [((3, ROWS, width), BF16, "lane"), ((2, ROWS, width), BF16, "lane")],
        [ext, rows, (8, LANES)],
    )
    taps_medium, taps_long, grad_filter, gain_total, grad_residue, grad_log = run(
        finish_kernel, "finish", width, [(last, "lane")],
        [((3, 3, width), F32, "lane"), ((3, 2, width), F32, "lane"), ((TAPS, width), F32, "lane"), ((1, width), F32, "lane"), ((MODES, MODES), F32, "whole"), ((MODES, MODES), F32, "whole")],
        [(SHARE * count + 8, LANES)], limit=16,
    )
    return (
        mixed,
        jnp.transpose(grad_med, (1, 0, 2)),
        jnp.transpose(grad_lng, (1, 0, 2)),
        taps_medium,
        taps_long,
        grad_filter,
        gain_total.reshape(width),
        grad_residue,
        grad_log,
    )


def solution(mesh):
    return jax.shard_map(
        on_device,
        mesh=mesh,
        in_specs=(
            P("ctx", None, "tp"),
            P("ctx", None, "tp"),
            P(None, None, "tp"),
            P(None, None, "tp"),
            P(None, "tp"),
            P("tp"),
            P(("tp", "ctx"), None),
            P(("tp", "ctx"), None),
            P("ctx", "tp"),
        ),
        out_specs=(
            P("ctx", "tp"),
            P("ctx", None, "tp"),
            P("ctx", None, "tp"),
            P(None, None, "tp"),
            P(None, None, "tp"),
            P(None, "tp"),
            P("tp"),
            P(("tp", "ctx"), None),
            P(("tp", "ctx"), None),
        ),
        check_vma=False,
    )
```

```python
import math

import jax
import jax.numpy as jnp
import ml_dtypes
import numpy as np
from jax import lax
from jax.experimental import pallas as pl
from jax.experimental.pallas import tpu as pltpu
from jax.sharding import PartitionSpec as P

D = 4096
MODES = 16
TAPS = 128
ROWS = 256
LANES = 128
CHUNKS = 8
STEPS = ROWS // CHUNKS
HALO = 144
WIDE = ROWS + TAPS
Q_END = TAPS
LONG_END = TAPS + 6
SHARE = 5
PAIRS = 16
HALF = SHARE * PAIRS
F32 = jnp.float32
BF16 = jnp.bfloat16
precise = lax.Precision.HIGHEST


def fourier_matrices():
    size = 2 * TAPS
    place = np.arange(size)
    mode = np.arange(TAPS)
    turn = 2.0 * math.pi / size
    cos_part = np.cos(turn * ((mode[:, None] * place[None, :]) % size))
    sin_part = -np.sin(turn * ((mode[:, None] * place[None, :]) % size))
    sin_part[0] = 1.0 - 2.0 * (place % 2)
    forward = np.concatenate([cos_part, sin_part], 0)
    weight = np.full((size,), 2.0 / size)
    weight[0] = weight[TAPS] = 1.0 / size
    backward = (forward * weight[:, None]).T

    return tuple(
        table.astype(ml_dtypes.bfloat16) for table in (forward, backward[:TAPS], backward[TAPS:])
    )


def f32_of(value):
    return value.astype(F32)


def rounded(value):
    return value.astype(BF16).astype(F32)


def spectrum(table, signal):
    return jnp.dot(table, signal, preferred_element_type=F32)


def from_spectrum(table, values):
    return jnp.dot(table, values.astype(BF16), preferred_element_type=F32)


def split_spectrum(values):
    real, imag = values[:TAPS], values[TAPS:]
    first = lax.broadcasted_iota(jnp.int32, real.shape, 0) == 0
    return real, jnp.where(first, imag, real), jnp.where(first, 0.0, imag)


def spread(value, row):
    return jnp.broadcast_to(value[row : row + 1, :], (CHUNKS, LANES))


def chunk_index():
    return lax.broadcasted_iota(jnp.int32, (CHUNKS, LANES), 0)


def at_step(ref, step):
    return ref[pl.ds(step, CHUNKS, stride=STEPS), :]


def chunk_states(source, rate, backward):
    decay = jnp.exp(-rate)
    decays = [spread(decay, r) for r in range(MODES)]

    def body(n, states):
        value = at_step(source, STEPS - 1 - n if backward else n)
        return tuple(decays[r] * states[r] + value for r in range(MODES))

    first = at_step(source, 0)
    return lax.fori_loop(0, STEPS, body, (first - first,) * MODES, unroll=4)


def powers(rate):
    return [jnp.exp(rate * float(-STEPS * by)) for by in (1, 2, 4)]


def chunk_entries(ends, power, backward):
    place = chunk_index()
    inside = [place < CHUNKS - by if backward else place >= by for by in (1, 2, 4)]
    entries = []
    for r in range(MODES):
        total = ends[r]
        for level, by in enumerate((1, 2, 4)):
            moved = pltpu.roll(total, CHUNKS - by if backward else by, 0)
            total = total + jnp.where(inside[level], spread(power[level], r) * moved, 0.0)
        moved = pltpu.roll(total, CHUNKS - 1 if backward else 1, 0)
        entries.append(jnp.where(inside[0], moved, 0.0))
    return entries


def chunk_weights(power, backward):
    after = chunk_index() if backward else CHUNKS - 1 - chunk_index()
    bits = [(after & by) != 0 for by in (1, 2, 4)]

    def weight(r):
        parts = [jnp.where(bit, spread(level, r), 1.0) for bit, level in zip(bits, power)]
        return parts[0] * parts[1] * parts[2]

    return weight, after.astype(F32) * float(STEPS)


def local_answer(source, target, rate, weight, entries, backward):
    decay = jnp.exp(-rate)
    decays = [spread(decay, r) for r in range(MODES)]
    weights = [spread(weight, r) for r in range(MODES)]

    def body(n, states):
        step = STEPS - 1 - n if backward else n
        value = at_step(source, step)
        states = tuple(decays[r] * states[r] + value for r in range(MODES))
        terms = [weights[r] * states[r] for r in range(MODES)]
        while len(terms) > 1:
            terms = [terms[k] + terms[k + 1] for k in range(0, len(terms), 2)]
        target[pl.ds(step, CHUNKS, stride=STEPS), :] = terms[0]
        return states

    lax.fori_loop(0, STEPS, body, tuple(entries), unroll=2)


def add_entry(local, target, rate, weight, entry, backward, inside=None):
    decay = jnp.exp(-rate)
    decays = [spread(decay, r) for r in range(MODES)]
    start = weight * entry
    factor, _ = chunk_weights(powers(rate), not backward)
    parts = [spread(start, r) * factor(r) for r in range(MODES)]
    if inside is not None:
        parts = [parts[r] + spread(weight, r) * inside[r] for r in range(MODES)]

    def body(n, parts):
        step = STEPS - 1 - n if backward else n
        parts = tuple(decays[r] * parts[r] for r in range(MODES))
        terms = list(parts)
        while len(terms) > 1:
            terms = [terms[k] + terms[k + 1] for k in range(0, len(terms), 2)]
        target[pl.ds(step, CHUNKS, stride=STEPS), :] = at_step(local, step) + terms[0]
        return parts

    lax.fori_loop(0, STEPS, body, tuple(parts), unroll=4)


def pair_state(early, late, rate, backward):
    near = jnp.exp(rate * float(-ROWS))
    return early + near * late if backward else near * early + late


def entry_state(gathered, other, rate, me, backward):
    far = jnp.exp(rate * float(-2 * ROWS))
    near = jnp.exp(rate * float(-ROWS))
    pair, second = me // 2, me % 2
    pairs = gathered.shape[0]

    def body(n, state):
        index = pairs - 1 - n if backward else n
        return far * state + gathered[index, 0:MODES, :].astype(F32)

    count = pairs - 1 - pair if backward else pair
    state = lax.fori_loop(0, count, body, jnp.zeros((MODES, LANES), F32))
    outer = second if backward else 1 - second
    return jnp.where(outer == 1, state, near * state + other)


def extend(ext, before, body):
    ext[6:8, :] = before
    ext[8 : 8 + ROWS, :] = body


def three(ext, taps):
    return (
        taps[0:1] * ext[8 : 8 + ROWS, :]
        + taps[1:2] * ext[7 : 7 + ROWS, :]
        + taps[2:3] * ext[6 : 6 + ROWS, :]
    )


def store_tap_sums(target, row, grad, ext):
    for shift in range(3):
        target[row + shift : row + shift + 1, :] = jnp.sum(
            grad * ext[8 - shift : 8 - shift + ROWS, :], 0, keepdims=True
        )


def tail_kernel(med, ends, taps, out, ext, rows):
    feats = []
    for j in (1, 2):
        extend(ext, jnp.zeros((2, LANES), F32), f32_of(med[j]))
        feats.append(rounded(three(ext, taps[j])))
    out[0:TAPS, :] = (feats[0][TAPS:] * feats[1][TAPS:]).astype(BF16)
    rows[...] = jnp.zeros(rows.shape, F32)
    for j in range(3):
        ext[8 : 8 + ROWS, :] = f32_of(med[j])
        rows[2 * j : 2 * j + 2, :] = ext[6 + ROWS : 8 + ROWS, :]
    rows[6:10, :] = ends[...]
    out[TAPS:HALO, :] = rows[...].astype(BF16)


def long_kernel(packed, before, lng, taps, cot, rate_out, weight_out, q_out, k_out, g_out, z_out, ends_out, ext, halo, grad, rows):
    both = jnp.transpose(packed[...].reshape(LANES, LANES))
    rate = jnp.exp(both[:MODES])
    rate_out[...] = rate
    weight_out[...] = both[MODES : 2 * MODES] * jnp.sqrt(2.0 * rate)
    halo[...] = f32_of(before[...])
    feats = []
    for j in range(2):
        extend(ext, halo[LONG_END + 2 * j : LONG_END + 2 * j + 2, :], f32_of(lng[j]))
        feats.append(three(ext, taps[j]).astype(BF16))
    q_out[...] = feats[0]
    k_out[...] = feats[1]
    sent = (f32_of(cot[...]) * f32_of(feats[0])).astype(BF16)
    g_out[...] = sent
    grad[...] = f32_of(sent)
    states = chunk_states(grad, rate, True)
    factor, _ = chunk_weights(powers(rate), True)
    for r in range(MODES):
        ends_out[r] = states[r]
        rows[r : r + 1, :] = jnp.sum(factor(r) * states[r], 0, keepdims=True)
    z_out[...] = rows[...].astype(BF16)


def join_kernel(me, own, other, rate, slot_out):
    first = me[0] % 2 == 0
    mine, theirs = f32_of(own[...]), f32_of(other[...])
    early, late = jnp.where(first, mine, theirs), jnp.where(first, theirs, mine)
    joined = pair_state(early, late, rate[...], True).astype(BF16)
    slot_out[...] = jnp.broadcast_to(joined[None], slot_out.shape)


def medium_kernel(med, before, taps, filt, forward, top,
                  prod_out, q_out, k_out, v_out, conv_out, gated_out, sq_out, ext, halo):
    halo[...] = f32_of(before[...])
    feats = []
    for j in range(3):
        extend(ext, halo[TAPS + 2 * j : TAPS + 2 * j + 2, :], f32_of(med[j]))
        feats.append(three(ext, taps[j]).astype(BF16))
    query, key, value = feats
    q_out[...] = query
    k_out[...] = key
    v_out[...] = value
    prod_out[0:TAPS, :] = before[0:TAPS, :]
    prod_out[TAPS:, :] = (f32_of(key) * f32_of(value)).astype(BF16)
    windows = jnp.concatenate([prod_out[0 : 2 * TAPS, :], prod_out[TAPS:, :]], 1)
    win = spectrum(forward[...], windows)
    ker = spectrum(forward[:, 0:TAPS], filt[...])
    ker_re, ker_alt, ker_im = split_spectrum(ker)
    ker_re, ker_alt, ker_im = (jnp.concatenate([k, k], 1) for k in (ker_re, ker_alt, ker_im))
    re, im = win[:TAPS], win[TAPS:]
    spec = jnp.concatenate([re * ker_re - im * ker_im, im * ker_alt + re * ker_im], 0)
    answer = from_spectrum(top[...], spec)
    conv = jnp.concatenate([answer[:, :LANES], answer[:, LANES:]], 0)
    conv_out[...] = conv
    gated = f32_of(query) * conv
    gated_out[...] = gated
    part = lax.dot_general(
        jnp.ones((8, LANES), F32), gated * gated, (((1,), (1,)), ((), ())),
        precision=precise, preferred_element_type=F32,
    )

    @pl.when(pl.program_id(0) == 0)
    def _():
        sq_out[...] = jnp.zeros(sq_out.shape, F32)

    sq_out[...] += part


def back_kernel(gconv, rate, weight, ends, y_out, grad):
    grad[...] = f32_of(gconv[...])
    entries = chunk_entries([ends[r] for r in range(MODES)], powers(rate[...]), True)
    local_answer(grad, y_out, rate[...], weight[...], entries, True)


def inner_kernel(me, zg, z_other, rate, weight, y_loc, k_two, gated, gain, square, gp_out, zin_out, in_out, full, total):
    entry = entry_state(zg, f32_of(z_other[...]), rate[...], me[0], True)
    zin_out[...] = entry
    add_entry(y_loc, full, rate[...], weight[...], entry, True)
    sent = full[...].astype(BF16)
    gp_out[...] = sent
    product = f32_of(sent) * f32_of(k_two[...]) * gain[...] * gated[...]
    part = lax.dot_general(
        jnp.ones((8, LANES), F32), product, (((1,), (1,)), ((), ())),
        precision=precise, preferred_element_type=F32,
    )

    @pl.when(pl.program_id(0) == 0)
    def _():
        total[...] = part

    @pl.when(pl.program_id(0) > 0)
    def _():
        total[...] += part

    @pl.when(pl.program_id(0) == pl.num_programs(0) - 1)
    def _():
        for device in range(in_out.shape[0]):
            in_out[device, 0:1, 0:ROWS] = square[0:1, :]
            in_out[device, 0:1, ROWS:] = total[0:1, :]


def norm_kernel(me, sums, gated, conv, q_one, k_one, v_one, k_two, gp, gain, filt, cot, prod, med, lng, before, rate, forward, low,
                x_out, gco_out, gq1_out, gk2_out, e_out, pair_out, keep_out, work, tail, ext, halo, f_out):
    ones = jnp.ones((8, LANES), F32)

    def column(values):
        return lax.dot_general(
            values, ones, (((0,), (0,)), ((), ())), precision=precise, preferred_element_type=F32
        )

    square = column(sums[:, 0, 0:ROWS]) / float(D) + 1e-06
    inner = column(sums[:, 0, ROWS:]) / float(D)
    scale = lax.rsqrt(square)
    gate = gated[...]
    key_two = f32_of(k_two[...])
    normed = rounded(gate * scale * gain[...])
    prod_two = (key_two * normed).astype(BF16)
    x_out[...] = prod_two
    grad_two = f32_of(gp[...])
    grad_k_two = grad_two * normed
    gk2_out[...] = grad_k_two
    grad_normed = grad_two * key_two
    f_out[TAPS:, :] = jnp.zeros((f_out.shape[0] - TAPS, LANES), F32)
    f_out[TAPS : TAPS + 1, :] = jnp.sum(grad_normed * gate * scale, 0, keepdims=True)
    grad_gated = scale * (grad_normed * gain[...] - gate * scale * scale * inner)
    grad_q_one = grad_gated * conv[...]
    gq1_out[...] = grad_q_one
    gco = (grad_gated * f32_of(q_one[...])).astype(BF16)
    gco_out[...] = gco
    e_out[0:TAPS, :] = gco[0:TAPS]
    tail[...] = jnp.zeros(tail.shape, F32)
    tail[0:2, :] = grad_q_one[0:2]
    work[...] = f32_of(gco)
    taps = f32_of(filt[...])
    for shift in range(2):
        head = jnp.sum(taps * work[shift : shift + TAPS, :], 0, keepdims=True)
        tail[2 + shift : 3 + shift, :] = head * f32_of(v_one[0:16, :])[shift : shift + 1]
        tail[4 + shift : 5 + shift, :] = head * f32_of(k_one[0:16, :])[shift : shift + 1]
    tail[6:8, :] = grad_k_two[0:2]
    tail[8:10, :] = f32_of(prod_two)[0:2]
    tail[10:12, :] = f32_of(cot[0:16, :])[0:2]
    e_out[TAPS:HALO, :] = tail[...].astype(BF16)
    halo[...] = f32_of(before[...])
    extend(ext, halo[Q_END : Q_END + 2, :], f32_of(med[0]))
    store_tap_sums(f_out, TAPS + 1, grad_q_one, ext)
    extend(ext, halo[LONG_END + 2 : LONG_END + 4, :], f32_of(lng[1]))
    store_tap_sums(f_out, TAPS + 4, grad_k_two, ext)
    win = spectrum(forward[...], jnp.concatenate([prod[0 : 2 * TAPS, :], prod[TAPS:, :]], 1))
    grd = spectrum(forward[:, TAPS:], jnp.concatenate([gco[0:TAPS], gco[TAPS:]], 1))
    win_re, win_alt, win_im = split_spectrum(win)
    re, im = grd[:TAPS], grd[TAPS:]
    spec = jnp.concatenate([re * win_re + im * win_im, im * win_alt - re * win_im], 0)
    f_out[0:TAPS, :] = from_spectrum(low[...], spec[:, :LANES] + spec[:, LANES:])
    work[...] = f32_of(prod_two)
    states = chunk_states(work, rate[...], False)
    factor, _ = chunk_weights(powers(rate[...]), False)
    for r in range(MODES):
        tail[r : r + 1, :] = jnp.sum(factor(r) * states[r], 0, keepdims=True)
    second = me[0] % 2
    pair_out[0:MODES, :] = tail[...].astype(BF16)
    pair_out[MODES:, :] = f_out[pl.ds(pl.multiple_of(HALF * (1 - second), 16), HALF), :].astype(BF16)
    keep_out[...] = f_out[pl.ds(pl.multiple_of(HALF * second, 16), HALF), :]


def share_kernel(me, pair, got, keep, rate, slot_out, add, slot):
    first = me[0] % 2 == 0
    mine, theirs = f32_of(pair[0:MODES, :]), f32_of(got[0:MODES, :])
    early, late = jnp.where(first, mine, theirs), jnp.where(first, theirs, mine)
    slot[0:MODES, :] = pair_state(early, late, rate[...], False)
    add[HALF:, :] = jnp.zeros((8, add.shape[1]), F32)
    add[0:HALF, :] = keep[...] + f32_of(got[MODES:, :])
    for device in range(slot_out.shape[0]):
        slot[MODES:, :] = add[SHARE * device : SHARE * device + 8, :]
        slot_out[device] = slot[...].astype(BF16)


def behind_kernel(g, rate, ends_out, gs):
    gs[...] = f32_of(g[...])
    decay = jnp.exp(-rate[...])
    first = at_step(gs, 0)
    zero = first - first
    half = MODES // 2
    for base in range(0, MODES, half):
        decays = [spread(decay, base + r) for r in range(half)]

        def behind(n, carry):
            z, q = carry
            grad = at_step(gs, STEPS - 1 - n)
            q = tuple(decays[r] * (q[r] + z[r]) for r in range(half))
            z = tuple(decays[r] * z[r] + grad for r in range(half))
            return z, q

        z, q = lax.fori_loop(0, STEPS, behind, ((zero,) * half,) * 2, unroll=4)
        for r in range(half):
            ends_out[base + r] = z[r]
            ends_out[MODES + base + r] = q[r]


def modes_kernel(x, g, rate, weight, ends, y_out, sums_out, entry_out, xs, gs):
    xs[...] = f32_of(x[...])
    gs[...] = f32_of(g[...])
    rates = rate[...]
    decay = jnp.exp(-rates)
    first = at_step(xs, 0)
    zero = first - first
    half = MODES // 2
    power = powers(rates)
    s_end, q_end, plain, slope = [], [], [], []
    z_end = [ends[r] for r in range(MODES)]
    zq_end = [ends[MODES + r] for r in range(MODES)]
    for base in range(0, MODES, half):
        decays = [spread(decay, base + r) for r in range(half)]
        weights = [spread(weight, base + r) for r in range(half)]

        def ahead(n, carry):
            s, q, p, l = carry
            value, grad = at_step(xs, n), at_step(gs, n)
            q = tuple(decays[r] * (q[r] + s[r]) for r in range(half))
            s = tuple(decays[r] * s[r] + value for r in range(half))
            p = tuple(p[r] + grad * s[r] for r in range(half))
            l = tuple(l[r] + grad * q[r] for r in range(half))
            terms = [weights[r] * s[r] for r in range(half)]
            while len(terms) > 1:
                terms = [terms[k] + terms[k + 1] for k in range(0, len(terms), 2)]
            answer = terms[0] if base == 0 else at_step(y_out, n) + terms[0]
            y_out[pl.ds(n, CHUNKS, stride=STEPS), :] = answer
            return s, q, p, l

        s, q, p, l = lax.fori_loop(0, STEPS, ahead, ((zero,) * half,) * 4, unroll=4)
        s_end += s
        q_end += q
        plain += p
        slope += l
    entries = chunk_entries(s_end, power, False)
    exits = chunk_entries(z_end, power, True)
    back, back_steps = chunk_weights(power, True)
    front, front_steps = chunk_weights(power, False)
    for r in range(MODES):
        a = spread(decay, r)
        a_step = a * spread(power[0], r)
        one = plain[r] + entries[r] * a * z_end[r]
        two = (
            slope[r]
            + float(STEPS) * a_step * entries[r] * exits[r]
            + a * (entries[r] * zq_end[r] + exits[r] * (q_end[r] + s_end[r]))
        )
        back_r, front_r = back(r), front(r)
        rows = (
            one,
            two,
            back_r * z_end[r],
            back_r * (zq_end[r] + back_steps * z_end[r]),
            front_r * (q_end[r] + s_end[r] + front_steps * s_end[r]),
        )
        for kind, value in enumerate(rows):
            place = kind * MODES + r
            sums_out[place : place + 1, :] = jnp.sum(value, 0, keepdims=True)
    for r in range(MODES):
        entry_out[r] = entries[r]


def kernel_spectrum(forward, filt, copies):
    parts = split_spectrum(spectrum(forward[:, 0:TAPS], filt[...]))
    return [jnp.concatenate([part] * copies, 1) if copies > 1 else part for part in parts]


def local_taps(gco, filt, k_one, v_one, med, before, forward, low, grad_out, taps_out, ext, halo):
    second = gco[TAPS:, :]
    pieces = jnp.concatenate(
        [gco[...], jnp.concatenate([second, jnp.zeros(second.shape, BF16)], 0)], 1
    )
    win = spectrum(forward[...], pieces)
    ker_re, ker_alt, ker_im = kernel_spectrum(forward, filt, 2)
    re, im = win[:TAPS], win[TAPS:]
    spec = jnp.concatenate([re * ker_re + im * ker_im, im * ker_alt - re * ker_im], 0)
    answer = from_spectrum(low[...], spec)
    grad_prod = jnp.concatenate([answer[:, :LANES], answer[:, LANES:]], 0)
    grad_out[...] = grad_prod
    halo[...] = f32_of(before[...])
    taps_out[...] = jnp.zeros(taps_out.shape, F32)
    for place, other in enumerate((v_one, k_one)):
        extend(ext, halo[TAPS + 2 + 2 * place : TAPS + 4 + 2 * place, :], f32_of(med[place + 1]))
        store_tap_sums(taps_out, 3 * place, grad_prod * f32_of(other[...]), ext)


def answer_kernel(me, sg, pair, other, rate, weight, y_loc, inside, q_two, cot, sums, zin, lng, before, tap_rows, after, filt, k_one, v_one, med, forward, low,
                  mixed_out, gq2_out, res_out, row_out, exit_out, late_out, ext, halo, full, rows):
    rates = rate[...]
    entry = entry_state(sg, f32_of(other[0:MODES, :]), rates, me[0], False)
    add_entry(y_loc, full, rates, weight[...], entry, False, inside)
    conv = rounded(full[...])
    grad_out = f32_of(cot[...])
    mixed_out[...] = (f32_of(q_two[...]) * conv).astype(BF16)
    grad_q_two = grad_out * conv
    gq2_out[...] = grad_q_two
    decay = jnp.exp(-rates)
    exit_out[...] = jnp.exp(rates * float(-ROWS)) * entry + f32_of(pair[0:MODES, :])
    plain = sums[0:MODES, :] + entry * decay * sums[2 * MODES : 3 * MODES, :]
    slope = (
        sums[MODES : 2 * MODES, :]
        + float(ROWS) * jnp.exp(rates * float(-ROWS - 1)) * entry * zin[...]
        + decay * (entry * sums[3 * MODES : 4 * MODES, :] + zin[...] * sums[4 * MODES :, :])
    )
    res_out[0:MODES, :] = (jnp.sqrt(2.0 * rates) * plain).astype(BF16)
    res_out[MODES:, :] = (weight[...] * (0.5 * plain - rates * slope)).astype(BF16)
    added = f32_of(sg[0])
    for device in range(1, sg.shape[0]):
        added = added + f32_of(sg[device])
    rows[0:8, :] = added[MODES : MODES + 8]
    rows[SHARE : SHARE + 6, :] = tap_rows[0:6, :]
    win = spectrum(forward[:, TAPS:], after[0:TAPS, :])
    ker_re, ker_alt, ker_im = kernel_spectrum(forward, filt, 1)
    re, im = win[:TAPS], win[TAPS:]
    spec = jnp.concatenate([re * ker_re + im * ker_im, im * ker_alt - re * ker_im], 0)
    late = from_spectrum(low[...], spec)
    late_out[...] = late
    for place, other in enumerate((v_one, k_one)):
        ext[0:ROWS, :] = f32_of(med[place + 1])
        grad = late * f32_of(other[TAPS:, :])
        for shift in range(3):
            row = SHARE + 3 * place + shift
            rows[row : row + 1, :] += jnp.sum(grad * ext[TAPS - shift : ROWS - shift, :], 0, keepdims=True)
    halo[...] = f32_of(before[TAPS:HALO, :])
    extend(ext, halo[6:8, :], f32_of(lng[0]))
    store_tap_sums(rows, SHARE + 6, grad_q_two, ext)
    row_out[...] = rows[...].astype(BF16)


def input_kernel(gq1, gpo, late, gq2, gk2, k_one, v_one, after, leave, rate, weight, mtaps, ltaps,
                 med_out, lng_out, ext, tail, nxt):
    tail[...] = f32_of(after[TAPS:HALO, :])
    grad_prod = jnp.concatenate([gpo[0:TAPS, :], gpo[TAPS:, :] + late[...]], 0)
    state = leave[...]
    decay = jnp.exp(-rate[...])
    for step in range(2):
        state = decay * state + tail[8 + step : 9 + step, :]
        value = rounded(jnp.sum(weight[...] * state, 0, keepdims=True))
        nxt[step : step + 1, :] = value * tail[10 + step : 11 + step, :]

    def back(grad, following, taps):
        ext[0:ROWS, :] = grad
        ext[ROWS : ROWS + 2, :] = following
        return (
            taps[0:1] * ext[0:ROWS, :] + taps[1:2] * ext[1 : ROWS + 1, :] + taps[2:3] * ext[2 : ROWS + 2, :]
        ).astype(BF16)

    med_out[0] = back(gq1[...], tail[0:2, :], mtaps[0])
    med_out[1] = back(grad_prod * f32_of(v_one[...]), tail[2:4, :], mtaps[1])
    med_out[2] = back(grad_prod * f32_of(k_one[...]), tail[4:6, :], mtaps[2])
    lng_out[0] = back(gq2[...], nxt[0:2, :], ltaps[0])
    lng_out[1] = back(gk2[...], tail[6:8, :], ltaps[1])


def last_kernel(me, every, mine, partner, slot_out, slot):
    first = me[0] % 2 == 0
    ours, others = f32_of(every[...]), f32_of(partner[...])
    slot[...] = jnp.zeros(slot.shape, F32)
    slot[0:SHARE, :] = jnp.where(first, ours[0:SHARE], others[0:SHARE])
    slot[SHARE : 2 * SHARE, :] = jnp.where(first, others[0:SHARE], ours[0:SHARE])
    slot[2 * SHARE : 2 * SHARE + 9, :] = ours[SHARE : SHARE + 9] + others[SHARE : SHARE + 9]
    own = f32_of(mine[...]) + others[MODES:]
    for pair in range(PAIRS):
        slot[2 * SHARE + 9 : 2 * SHARE + 10, :] = own[pair : pair + 1]
        slot_out[pair] = slot[...].astype(BF16)


def finish_kernel(last, mtap_out, ltap_out, filt_out, gain_out, res_out, log_out, f_all):
    added = jnp.zeros((last.shape[1], LANES), F32)
    for pair in range(PAIRS):
        piece = f32_of(last[pair])
        f_all[SHARE * pair : SHARE * pair + 8, :] = piece[0:8]
        added = added + piece
    for pair in range(PAIRS):
        start = HALF + SHARE * pair
        f_all[start : start + 8, :] = f32_of(last[pair])[SHARE : SHARE + 8]
    filt_out[...] = f_all[0:TAPS, :]
    gain_out[...] = f_all[TAPS : TAPS + 1, :]
    for shift in range(3):
        mtap_out[shift, 0:1, :] = f_all[TAPS + 1 + shift : TAPS + 2 + shift, :]
        ltap_out[shift, 1:2, :] = f_all[TAPS + 4 + shift : TAPS + 5 + shift, :]
        mtap_out[shift, 1:2, :] = added[2 * SHARE + shift : 2 * SHARE + 1 + shift]
        mtap_out[shift, 2:3, :] = added[2 * SHARE + 3 + shift : 2 * SHARE + 4 + shift]
        ltap_out[shift, 0:1, :] = added[2 * SHARE + 6 + shift : 2 * SHARE + 7 + shift]
    block = pl.program_id(0)
    lane = lax.broadcasted_iota(jnp.int32, (MODES, LANES), 1)
    row = lax.broadcasted_iota(jnp.int32, (MODES, LANES), 0)
    picked = jnp.where(lane % MODES == row, added[2 * SHARE + 9 : 2 * SHARE + 10], 0.0)
    goal = (row == lane // MODES + 8 * (block % 2)).astype(F32)
    part = lax.dot_general(
        picked, goal, (((1,), (1,)), ((), ())), precision=precise, preferred_element_type=F32
    )

    @pl.when(block == 0)
    def _():
        res_out[...] = part

    @pl.when(block == 1)
    def _():
        res_out[...] += part

    @pl.when(block == 2)
    def _():
        log_out[...] = part

    @pl.when(block == 3)
    def _():
        log_out[...] += part


def block_of(shape, kind, lanes):
    if kind == "lane":
        lead = shape[:-1]
        return pl.BlockSpec(lead + (lanes,), lambda l: (0,) * len(lead) + (l,))
    if kind == "whole":
        return pl.BlockSpec(shape, lambda l: (0,) * len(shape))
    if kind == "source":
        return pl.BlockSpec((8,) + shape[1:], lambda l: (l,) + (0,) * (len(shape) - 1))
    return pl.BlockSpec(memory_space=pltpu.SMEM)


def run(kernel, name, width, inputs, outputs, scratch, limit=63, flops=1000000, lanes=LANES):
    arrays = [array for array, _ in inputs]
    moved = sum(a.size * a.dtype.itemsize for a in arrays)
    return pl.pallas_call(
        kernel,
        grid=(width // lanes,),
        in_specs=[block_of(a.shape, kind, lanes) for a, kind in inputs],
        out_specs=[block_of(shape, kind, lanes) for shape, _, kind in outputs],
        out_shape=[
            jax.ShapeDtypeStruct(shape, dtype) for shape, dtype, _ in outputs
        ],
        scratch_shapes=[pltpu.VMEM(shape, F32) for shape in scratch],
        compiler_params=pltpu.CompilerParams(vmem_limit_bytes=limit * 1024 * 1024),
        cost_estimate=pl.CostEstimate(flops=flops, bytes_accessed=moved, transcendentals=0),
        name=name,
    )(*arrays)


def passed_along(array, axis, by):
    count = lax.axis_size(axis)
    pairs = [(i, i + by) for i in range(count) if 0 <= i + by < count]
    return lax.ppermute(array, axis, pairs)


def exchanged(array):
    return lax.ppermute(array, "ctx", [(i, i ^ 1) for i in range(lax.axis_size("ctx"))])


def in_plane(array):
    groups = [[2 * p + z for p in range(PAIRS)] for z in range(2)]
    return lax.all_to_all(array, "ctx", split_axis=0, concat_axis=0, tiled=True, axis_index_groups=groups)


def swap(array, axis):
    return lax.all_to_all(array, axis, split_axis=0, concat_axis=0, tiled=True)


def on_device(medium_input, long_input, medium_taps, long_taps, medium_filter, norm_gain, long_residue, long_log_decay, cotangent):
    width = cotangent.shape[1]
    count = lax.axis_size("ctx")
    me = lax.axis_index("ctx").astype(jnp.int32).reshape(1)
    forward, low, top = (jnp.asarray(table) for table in fourier_matrices())
    med = jnp.transpose(medium_input, (1, 0, 2))
    lng = jnp.transpose(long_input, (1, 0, 2))
    mtaps = jnp.transpose(medium_taps, (1, 0, 2))
    ltaps = jnp.transpose(long_taps, (1, 0, 2))
    gain = norm_gain.reshape(1, width)
    filt = medium_filter
    ext = (ROWS + 8, LANES)
    halo = (HALO, LANES)
    wide = (WIDE, width)
    full = (ROWS, LANES)
    rows = (MODES, LANES)
    plane = (ROWS, width)
    modes = (MODES, width)

    mine = jnp.pad(jnp.concatenate([long_log_decay, long_residue], 1), ((0, 0), (0, LANES - 2 * MODES)))
    packed = swap(jnp.broadcast_to(mine[None], (count,) + mine.shape), "ctx")

    ends = jnp.transpose(long_input[ROWS - 2 :].astype(F32), (1, 0, 2)).reshape(4, width)
    (tail,) = run(
        tail_kernel, "tail", width, [(med, "lane"), (ends, "lane"), (mtaps, "lane")],
        [((HALO, width), BF16, "lane")], [ext, rows], limit=16,
    )
    before = passed_along(tail, "ctx", 1)

    rate, weight, q_two, k_two, gconv, z_all, z_ends = run(
        long_kernel, "long", width,
        [(packed, "source"), (before, "lane"), (lng, "lane"), (ltaps, "lane"), (cotangent, "lane")],
        [(modes, F32, "lane"), (modes, F32, "lane"), (plane, BF16, "lane"), (plane, BF16, "lane"), (plane, BF16, "lane"), (modes, BF16, "lane"), ((MODES, CHUNKS, width), F32, "lane")],
        [ext, halo, full, rows],
    )
    z_other = exchanged(z_all)
    prod, q_one, k_one, v_one, conv, gated, square = run(
        medium_kernel, "medium", width,
        [(med, "lane"), (before, "lane"), (mtaps, "lane"), (filt, "lane"), (forward, "whole"), (top, "whole")],
        [(wide, BF16, "lane"), (plane, BF16, "lane"), (plane, BF16, "lane"), (plane, BF16, "lane"), (plane, F32, "lane"), (plane, F32, "lane"), ((8, ROWS), F32, "whole")],
        [ext, halo],
    )
    z_other, square = lax.optimization_barrier((z_other, square))
    (z_pairs,) = run(
        join_kernel, "join", width, [(me, "scalar"), (z_all, "lane"), (z_other, "lane"), (rate, "lane")],
        [((PAIRS,) + modes, BF16, "lane")], [], lanes=width,
    )
    zg = in_plane(z_pairs)
    (y_back,) = run(
        back_kernel, "back", width,
        [(gconv, "lane"), (rate, "lane"), (weight, "lane"), (z_ends, "lane")],
        [(plane, F32, "lane")], [full],
    )
    grad_prod, zin, inner = run(
        inner_kernel, "inner", width,
        [(me, "scalar"), (zg, "lane"), (z_other, "lane"), (rate, "lane"), (weight, "lane"), (y_back, "lane"), (k_two, "lane"), (gated, "lane"), (gain, "lane"), (square, "whole")],
        [(plane, BF16, "lane"), (modes, F32, "lane"), ((8, 1, 2 * ROWS), F32, "whole")],
        [full, (8, ROWS)],
    )
    sums = swap(inner, "tp")
    later, _ = lax.optimization_barrier((gconv, inner))
    (ends_back,) = run(
        behind_kernel, "behind", width, [(later, "lane"), (rate, "lane")],
        [((2 * MODES, CHUNKS, width), F32, "lane")], [full],
    )
    sums, ends_back = lax.optimization_barrier((sums, ends_back))

    x, gco, gq1, gk2, edge, pair, keep = run(
        norm_kernel, "norm", width,
        [(me, "scalar"), (sums, "whole"), (gated, "lane"), (conv, "lane"), (q_one, "lane"), (k_one, "lane"), (v_one, "lane"), (k_two, "lane"), (grad_prod, "lane"), (gain, "lane"), (filt, "lane"), (cotangent, "lane"), (prod, "lane"), (med, "lane"), (lng, "lane"), (before, "lane"), (rate, "lane"), (forward, "whole"), (low, "whole")],
        [(plane, BF16, "lane"), (plane, BF16, "lane"), (plane, F32, "lane"), (plane, F32, "lane"), ((HALO, width), BF16, "lane"), ((MODES + HALF, width), BF16, "lane"), ((HALF, width), F32, "lane")],
        [full, rows, ext, halo, (2 * HALF, LANES)],
    )
    other = exchanged(pair)
    gpo, tap_rows = run(
        local_taps, "taps", width,
        [(gco, "lane"), (filt, "lane"), (k_one, "lane"), (v_one, "lane"), (med, "lane"), (before, "lane"), (forward, "whole"), (low, "whole")],
        [(plane, F32, "lane"), ((8, width), F32, "lane")], [ext, halo],
    )
    edge, tap_rows = lax.optimization_barrier((edge, tap_rows))
    after = passed_along(edge, "ctx", -1)
    other, tap_rows = lax.optimization_barrier((other, tap_rows))
    (sent,) = run(
        share_kernel, "share", width,
        [(me, "scalar"), (pair, "lane"), (other, "lane"), (keep, "lane"), (rate, "lane")],
        [((PAIRS, MODES + 8, width), BF16, "lane")], [(HALF + 8, width), (MODES + 8, width)], lanes=width,
    )
    got = in_plane(sent)

    y_front, mode_sums, inside = run(
        modes_kernel, "modes", width,
        [(x, "lane"), (gconv, "lane"), (rate, "lane"), (weight, "lane"), (ends_back, "lane")],
        [(plane, F32, "lane"), ((5 * MODES, width), F32, "lane"), ((MODES, CHUNKS, width), F32, "lane")], [full, full],
    )
    mixed, gq2, res, every, leave, late = run(
        answer_kernel, "answer", width,
        [(me, "scalar"), (got, "lane"), (pair, "lane"), (other, "lane"), (rate, "lane"), (weight, "lane"), (y_front, "lane"), (inside, "lane"), (q_two, "lane"), (cotangent, "lane"), (mode_sums, "lane"), (zin, "lane"), (lng, "lane"), (before, "lane"), (tap_rows, "lane"), (after, "lane"), (filt, "lane"), (k_one, "lane"), (v_one, "lane"), (med, "lane"), (forward, "whole"), (low, "whole")],
        [(plane, BF16, "lane"), (plane, F32, "lane"), ((2 * MODES, width), BF16, "lane"), ((MODES, width), BF16, "lane"), (modes, F32, "lane"), ((TAPS, width), F32, "lane")],
        [ext, rows, full, rows],
    )
    own = res.reshape(2 * MODES, PAIRS, 2, MODES).transpose(2, 1, 0, 3).reshape(2, PAIRS, width)
    second = me[0] % 2
    mine = lax.dynamic_index_in_dim(own, second, 0, keepdims=False)
    theirs = lax.dynamic_index_in_dim(own, 1 - second, 0, keepdims=False)
    partner = exchanged(jnp.concatenate([every, theirs], 0))
    (slots,) = run(
        last_kernel, "last", width,
        [(me, "scalar"), (every, "lane"), (mine, "lane"), (partner, "lane")],
        [((PAIRS, 24, width), BF16, "lane")], [(24, width)], lanes=width,
    )
    last = in_plane(slots)

    grad_med, grad_lng = run(
        input_kernel, "inputs", width,
        [(gq1, "lane"), (gpo, "lane"), (late, "lane"), (gq2, "lane"), (gk2, "lane"), (k_one, "lane"), (v_one, "lane"), (after, "lane"), (leave, "lane"), (rate, "lane"), (weight, "lane"), (mtaps, "lane"), (ltaps, "lane")],
        [((3, ROWS, width), BF16, "lane"), ((2, ROWS, width), BF16, "lane")],
        [ext, rows, (8, LANES)],
    )
    taps_medium, taps_long, grad_filter, gain_total, grad_residue, grad_log = run(
        finish_kernel, "finish", width, [(last, "lane")],
        [((3, 3, width), F32, "lane"), ((3, 2, width), F32, "lane"), ((TAPS, width), F32, "lane"), ((1, width), F32, "lane"), ((MODES, MODES), F32, "whole"), ((MODES, MODES), F32, "whole")],
        [(SHARE * count + 8, LANES)], limit=16,
    )
    return (
        mixed,
        jnp.transpose(grad_med, (1, 0, 2)),
        jnp.transpose(grad_lng, (1, 0, 2)),
        taps_medium,
        taps_long,
        grad_filter,
        gain_total.reshape(width),
        grad_residue,
        grad_log,
    )


def solution(mesh):
    return jax.shard_map(
        on_device,
        mesh=mesh,
        in_specs=(
            P("ctx", None, "tp"),
            P("ctx", None, "tp"),
            P(None, None, "tp"),
            P(None, None, "tp"),
            P(None, "tp"),
            P("tp"),
            P(("tp", "ctx"), None),
            P(("tp", "ctx"), None),
            P("ctx", "tp"),
        ),
        out_specs=(
            P("ctx", "tp"),
            P("ctx", None, "tp"),
            P("ctx", None, "tp"),
            P(None, None, "tp"),
            P(None, None, "tp"),
            P(None, "tp"),
            P("tp"),
            P(("tp", "ctx"), None),
            P(("tp", "ctx"), None),
        ),
        check_vma=False,
    )
```

```python
import math

import jax
import jax.numpy as jnp
import ml_dtypes
import numpy as np
from jax import lax
from jax.experimental import pallas as pl
from jax.experimental.pallas import tpu as pltpu
from jax.sharding import PartitionSpec as P

D = 4096
MODES = 16
TAPS = 128
ROWS = 256
LANES = 128
CHUNKS = 8
STEPS = ROWS // CHUNKS
HALO = 144
WIDE = ROWS + TAPS
Q_END = TAPS
LONG_END = TAPS + 6
SHARE = 5
PAIRS = 16
HALF = SHARE * PAIRS
F32 = jnp.float32
BF16 = jnp.bfloat16
precise = lax.Precision.HIGHEST


def fourier_matrices():
    size = 2 * TAPS
    place = np.arange(size)
    mode = np.arange(TAPS)
    turn = 2.0 * math.pi / size
    cos_part = np.cos(turn * ((mode[:, None] * place[None, :]) % size))
    sin_part = -np.sin(turn * ((mode[:, None] * place[None, :]) % size))
    sin_part[0] = 1.0 - 2.0 * (place % 2)
    forward = np.concatenate([cos_part, sin_part], 0)
    weight = np.full((size,), 2.0 / size)
    weight[0] = weight[TAPS] = 1.0 / size
    backward = (forward * weight[:, None]).T

    return tuple(
        table.astype(ml_dtypes.bfloat16) for table in (forward, backward[:TAPS], backward[TAPS:])
    )


def f32_of(value):
    return value.astype(F32)


def rounded(value):
    return value.astype(BF16).astype(F32)


def spectrum(table, signal):
    return jnp.dot(table, signal, preferred_element_type=F32)


def from_spectrum(table, values):
    return jnp.dot(table, values.astype(BF16), preferred_element_type=F32)


def split_spectrum(values):
    real, imag = values[:TAPS], values[TAPS:]
    first = lax.broadcasted_iota(jnp.int32, real.shape, 0) == 0
    return real, jnp.where(first, imag, real), jnp.where(first, 0.0, imag)


def spread(value, row):
    return jnp.broadcast_to(value[row : row + 1, :], (CHUNKS, LANES))


def chunk_index():
    return lax.broadcasted_iota(jnp.int32, (CHUNKS, LANES), 0)


def at_step(ref, step):
    return ref[pl.ds(step, CHUNKS, stride=STEPS), :]


def chunk_states(source, rate, backward):
    decay = jnp.exp(-rate)
    decays = [spread(decay, r) for r in range(MODES)]

    def body(n, states):
        value = at_step(source, STEPS - 1 - n if backward else n)
        return tuple(decays[r] * states[r] + value for r in range(MODES))

    first = at_step(source, 0)
    return lax.fori_loop(0, STEPS, body, (first - first,) * MODES, unroll=4)


def powers(rate):
    return [jnp.exp(rate * float(-STEPS * by)) for by in (1, 2, 4)]


def chunk_entries(ends, power, backward):
    place = chunk_index()
    inside = [place < CHUNKS - by if backward else place >= by for by in (1, 2, 4)]
    entries = []
    for r in range(MODES):
        total = ends[r]
        for level, by in enumerate((1, 2, 4)):
            moved = pltpu.roll(total, CHUNKS - by if backward else by, 0)
            total = total + jnp.where(inside[level], spread(power[level], r) * moved, 0.0)
        moved = pltpu.roll(total, CHUNKS - 1 if backward else 1, 0)
        entries.append(jnp.where(inside[0], moved, 0.0))
    return entries


def chunk_weights(power, backward):
    after = chunk_index() if backward else CHUNKS - 1 - chunk_index()
    bits = [(after & by) != 0 for by in (1, 2, 4)]

    def weight(r):
        parts = [jnp.where(bit, spread(level, r), 1.0) for bit, level in zip(bits, power)]
        return parts[0] * parts[1] * parts[2]

    return weight, after.astype(F32) * float(STEPS)


def local_answer(source, target, rate, weight, entries, backward):
    decay = jnp.exp(-rate)
    decays = [spread(decay, r) for r in range(MODES)]
    weights = [spread(weight, r) for r in range(MODES)]

    def body(n, states):
        step = STEPS - 1 - n if backward else n
        value = at_step(source, step)
        states = tuple(decays[r] * states[r] + value for r in range(MODES))
        terms = [weights[r] * states[r] for r in range(MODES)]
        while len(terms) > 1:
            terms = [terms[k] + terms[k + 1] for k in range(0, len(terms), 2)]
        target[pl.ds(step, CHUNKS, stride=STEPS), :] = terms[0]
        return states

    lax.fori_loop(0, STEPS, body, tuple(entries), unroll=2)


def add_entry(target, rate, weight, entry, backward, inside=None):
    decay = jnp.exp(-rate)
    decays = [spread(decay, r) for r in range(MODES)]
    start = weight * entry
    factor, _ = chunk_weights(powers(rate), not backward)
    parts = [spread(start, r) * factor(r) for r in range(MODES)]
    if inside is not None:
        parts = [parts[r] + spread(weight, r) * inside[r] for r in range(MODES)]

    def body(n, parts):
        step = STEPS - 1 - n if backward else n
        parts = tuple(decays[r] * parts[r] for r in range(MODES))
        terms = list(parts)
        while len(terms) > 1:
            terms = [terms[k] + terms[k + 1] for k in range(0, len(terms), 2)]
        target[pl.ds(step, CHUNKS, stride=STEPS), :] = at_step(target, step) + terms[0]
        return parts

    lax.fori_loop(0, STEPS, body, tuple(parts), unroll=4)


def pair_state(early, late, rate, backward):
    near = jnp.exp(rate * float(-ROWS))
    return early + near * late if backward else near * early + late


def entry_state(gathered, other, rate, me, backward):
    far = jnp.exp(rate * float(-2 * ROWS))
    near = jnp.exp(rate * float(-ROWS))
    pair, second = me // 2, me % 2
    pairs = gathered.shape[0]

    def body(n, state):
        index = pairs - 1 - n if backward else n
        return far * state + gathered[index, 0:MODES, :].astype(F32)

    count = pairs - 1 - pair if backward else pair
    state = lax.fori_loop(0, count, body, jnp.zeros((MODES, LANES), F32))
    outer = second if backward else 1 - second
    return jnp.where(outer == 1, state, near * state + other)


def extend(ext, before, body):
    ext[6:8, :] = before
    ext[8 : 8 + ROWS, :] = body


def three(ext, taps):
    return (
        taps[0:1] * ext[8 : 8 + ROWS, :]
        + taps[1:2] * ext[7 : 7 + ROWS, :]
        + taps[2:3] * ext[6 : 6 + ROWS, :]
    )


def store_tap_sums(target, row, grad, ext):
    for shift in range(3):
        target[row + shift : row + shift + 1, :] = jnp.sum(
            grad * ext[8 - shift : 8 - shift + ROWS, :], 0, keepdims=True
        )


def tail_kernel(med, ends, taps, out, ext, rows):
    feats = []
    for j in (1, 2):
        extend(ext, jnp.zeros((2, LANES), F32), f32_of(med[j]))
        feats.append(rounded(three(ext, taps[j])))
    out[0:TAPS, :] = (feats[0][TAPS:] * feats[1][TAPS:]).astype(BF16)
    rows[...] = jnp.zeros(rows.shape, F32)
    for j in range(3):
        ext[8 : 8 + ROWS, :] = f32_of(med[j])
        rows[2 * j : 2 * j + 2, :] = ext[6 + ROWS : 8 + ROWS, :]
    rows[6:10, :] = ends[...]
    out[TAPS:HALO, :] = rows[...].astype(BF16)


def long_kernel(packed, before, lng, taps, cot, rate_out, weight_out, q_out, k_out, g_out, z_out, ends_out, ext, halo, grad, rows):
    both = jnp.transpose(packed[...].reshape(LANES, LANES))
    rate = jnp.exp(both[:MODES])
    rate_out[...] = rate
    weight_out[...] = both[MODES : 2 * MODES] * jnp.sqrt(2.0 * rate)
    halo[...] = f32_of(before[...])
    feats = []
    for j in range(2):
        extend(ext, halo[LONG_END + 2 * j : LONG_END + 2 * j + 2, :], f32_of(lng[j]))
        feats.append(three(ext, taps[j]).astype(BF16))
    q_out[...] = feats[0]
    k_out[...] = feats[1]
    sent = (f32_of(cot[...]) * f32_of(feats[0])).astype(BF16)
    g_out[...] = sent
    grad[...] = f32_of(sent)
    states = chunk_states(grad, rate, True)
    factor, _ = chunk_weights(powers(rate), True)
    for r in range(MODES):
        ends_out[r] = states[r]
        rows[r : r + 1, :] = jnp.sum(factor(r) * states[r], 0, keepdims=True)
    z_out[...] = rows[...].astype(BF16)


def join_kernel(me, own, other, rate, slot_out):
    first = me[0] % 2 == 0
    mine, theirs = f32_of(own[...]), f32_of(other[...])
    early, late = jnp.where(first, mine, theirs), jnp.where(first, theirs, mine)
    joined = pair_state(early, late, rate[...], True).astype(BF16)
    slot_out[...] = jnp.broadcast_to(joined[None], slot_out.shape)


def medium_kernel(med, before, taps, filt, forward, top,
                  prod_out, q_out, k_out, v_out, conv_out, gated_out, sq_out, ext, halo, block):
    halo[...] = f32_of(before[...])
    feats = []
    for j in range(3):
        extend(ext, halo[TAPS + 2 * j : TAPS + 2 * j + 2, :], f32_of(med[j]))
        feats.append(three(ext, taps[j]).astype(BF16))
    query, key, value = feats
    q_out[...] = query
    k_out[...] = key
    v_out[...] = value
    prod_out[0:TAPS, :] = before[0:TAPS, :]
    prod_out[TAPS:, :] = (f32_of(key) * f32_of(value)).astype(BF16)
    windows = jnp.concatenate([prod_out[0 : 2 * TAPS, :], prod_out[TAPS:, :]], 1)
    win = spectrum(forward[...], windows)
    ker = spectrum(forward[:, 0:TAPS], filt[...])
    ker_re, ker_alt, ker_im = split_spectrum(ker)
    ker_re, ker_alt, ker_im = (jnp.concatenate([k, k], 1) for k in (ker_re, ker_alt, ker_im))
    re, im = win[:TAPS], win[TAPS:]
    spec = jnp.concatenate([re * ker_re - im * ker_im, im * ker_alt + re * ker_im], 0)
    answer = from_spectrum(top[...], spec)
    conv = jnp.concatenate([answer[:, :LANES], answer[:, LANES:]], 0)
    conv_out[...] = conv
    gated = f32_of(query) * conv
    gated_out[...] = gated
    part = lax.dot_general(
        jnp.ones((8, LANES), F32), gated * gated, (((1,), (1,)), ((), ())),
        precision=precise, preferred_element_type=F32,
    )

    if block == 0:
        sq_out[...] = part
    else:
        sq_out[...] += part


def back_kernel(gconv, rate, weight, ends, y_out, grad, full):
    grad[...] = f32_of(gconv[...])
    entries = chunk_entries([ends[r] for r in range(MODES)], powers(rate[...]), True)
    local_answer(grad, full, rate[...], weight[...], entries, True)
    y_out[...] = full[...]


def inner_kernel(me, zg, z_other, rate, weight, y_loc, k_two, gated, gain, square, gp_out, zin_out, in_out, full, total):
    entry = entry_state(zg, f32_of(z_other[...]), rate[...], me[0], True)
    zin_out[...] = entry
    full[...] = y_loc[...]
    add_entry(full, rate[...], weight[...], entry, True)
    sent = full[...].astype(BF16)
    gp_out[...] = sent
    product = f32_of(sent) * f32_of(k_two[...]) * gain[...] * gated[...]
    part = lax.dot_general(
        jnp.ones((8, LANES), F32), product, (((1,), (1,)), ((), ())),
        precision=precise, preferred_element_type=F32,
    )

    block = pl.program_id(0)

    @pl.when(block == 0)
    def _():
        total[...] = part

    @pl.when(block > 0)
    def _():
        total[...] += part

    @pl.when(block == pl.num_programs(0) - 1)
    def _():
        for device in range(in_out.shape[0]):
            in_out[device, 0:1, 0:ROWS] = square[0:1, :]
            in_out[device, 0:1, ROWS:] = total[0:1, :]


def norm_kernel(me, sums, gated, conv, q_one, k_one, v_one, k_two, gp, gain, filt, cot, prod, med, lng, before, rate, forward, low,
                x_out, gco_out, gq1_out, gk2_out, e_out, pair_out, keep_out, work, tail, ext, halo, f_out):
    ones = jnp.ones((8, LANES), F32)

    def column(values):
        return lax.dot_general(
            values, ones, (((0,), (0,)), ((), ())), precision=precise, preferred_element_type=F32
        )

    square = column(sums[:, 0, 0:ROWS]) / float(D) + 1e-06
    inner = column(sums[:, 0, ROWS:]) / float(D)
    scale = lax.rsqrt(square)
    gate = gated[...]
    key_two = f32_of(k_two[...])
    normed = rounded(gate * scale * gain[...])
    prod_two = (key_two * normed).astype(BF16)
    x_out[...] = prod_two
    grad_two = f32_of(gp[...])
    grad_k_two = grad_two * normed
    gk2_out[...] = grad_k_two
    grad_normed = grad_two * key_two
    f_out[TAPS:, :] = jnp.zeros((f_out.shape[0] - TAPS, LANES), F32)
    f_out[TAPS : TAPS + 1, :] = jnp.sum(grad_normed * gate * scale, 0, keepdims=True)
    grad_gated = scale * (grad_normed * gain[...] - gate * scale * scale * inner)
    grad_q_one = grad_gated * conv[...]
    gq1_out[...] = grad_q_one
    gco = (grad_gated * f32_of(q_one[...])).astype(BF16)
    gco_out[...] = gco
    e_out[0:TAPS, :] = gco[0:TAPS]
    tail[...] = jnp.zeros(tail.shape, F32)
    tail[0:2, :] = grad_q_one[0:2]
    work[...] = f32_of(gco)
    taps = f32_of(filt[...])
    for shift in range(2):
        head = jnp.sum(taps * work[shift : shift + TAPS, :], 0, keepdims=True)
        tail[2 + shift : 3 + shift, :] = head * f32_of(v_one[0:16, :])[shift : shift + 1]
        tail[4 + shift : 5 + shift, :] = head * f32_of(k_one[0:16, :])[shift : shift + 1]
    tail[6:8, :] = grad_k_two[0:2]
    tail[8:10, :] = f32_of(prod_two)[0:2]
    tail[10:12, :] = f32_of(cot[0:16, :])[0:2]
    e_out[TAPS:HALO, :] = tail[...].astype(BF16)
    halo[...] = f32_of(before[...])
    extend(ext, halo[Q_END : Q_END + 2, :], f32_of(med[0]))
    store_tap_sums(f_out, TAPS + 1, grad_q_one, ext)
    extend(ext, halo[LONG_END + 2 : LONG_END + 4, :], f32_of(lng[1]))
    store_tap_sums(f_out, TAPS + 4, grad_k_two, ext)
    win = spectrum(forward[...], jnp.concatenate([prod[0 : 2 * TAPS, :], prod[TAPS:, :]], 1))
    grd = spectrum(forward[:, TAPS:], jnp.concatenate([gco[0:TAPS], gco[TAPS:]], 1))
    win_re, win_alt, win_im = split_spectrum(win)
    re, im = grd[:TAPS], grd[TAPS:]
    spec = jnp.concatenate([re * win_re + im * win_im, im * win_alt - re * win_im], 0)
    f_out[0:TAPS, :] = from_spectrum(low[...], spec[:, :LANES] + spec[:, LANES:])
    work[...] = f32_of(prod_two)
    states = chunk_states(work, rate[...], False)
    factor, _ = chunk_weights(powers(rate[...]), False)
    for r in range(MODES):
        tail[r : r + 1, :] = jnp.sum(factor(r) * states[r], 0, keepdims=True)
    second = me[0] % 2
    pair_out[0:MODES, :] = tail[...].astype(BF16)
    pair_out[MODES:, :] = f_out[pl.ds(pl.multiple_of(HALF * (1 - second), 16), HALF), :].astype(BF16)
    keep_out[...] = f_out[pl.ds(pl.multiple_of(HALF * second, 16), HALF), :]


def share_kernel(me, pair, got, keep, rate, slot_out, add, slot):
    first = me[0] % 2 == 0
    mine, theirs = f32_of(pair[0:MODES, :]), f32_of(got[0:MODES, :])
    early, late = jnp.where(first, mine, theirs), jnp.where(first, theirs, mine)
    slot[0:MODES, :] = pair_state(early, late, rate[...], False)
    add[HALF:, :] = jnp.zeros((8, add.shape[1]), F32)
    add[0:HALF, :] = keep[...] + f32_of(got[MODES:, :])
    for device in range(slot_out.shape[0]):
        slot[MODES:, :] = add[SHARE * device : SHARE * device + 8, :]
        slot_out[device] = slot[...].astype(BF16)


def behind_kernel(g, rate, ends_out, gs):
    gs[...] = f32_of(g[...])
    decay = jnp.exp(-rate[...])
    first = at_step(gs, 0)
    zero = first - first
    half = MODES // 2
    for base in range(0, MODES, half):
        decays = [spread(decay, base + r) for r in range(half)]

        def behind(n, carry):
            z, q = carry
            grad = at_step(gs, STEPS - 1 - n)
            q = tuple(decays[r] * (q[r] + z[r]) for r in range(half))
            z = tuple(decays[r] * z[r] + grad for r in range(half))
            return z, q

        z, q = lax.fori_loop(0, STEPS, behind, ((zero,) * half,) * 2, unroll=4)
        for r in range(half):
            ends_out[base + r] = z[r]
            ends_out[MODES + base + r] = q[r]


def modes_kernel(x, g, rate, weight, ends, y_out, sums_out, entry_out, xs, gs, full):
    xs[...] = f32_of(x[...])
    gs[...] = f32_of(g[...])
    rates = rate[...]
    decay = jnp.exp(-rates)
    first = at_step(xs, 0)
    zero = first - first
    half = MODES // 2
    power = powers(rates)
    s_end, q_end, plain, slope = [], [], [], []
    z_end = [ends[r] for r in range(MODES)]
    zq_end = [ends[MODES + r] for r in range(MODES)]
    for base in range(0, MODES, half):
        decays = [spread(decay, base + r) for r in range(half)]
        weights = [spread(weight, base + r) for r in range(half)]

        def ahead(n, carry):
            s, q, p, l = carry
            value, grad = at_step(xs, n), at_step(gs, n)
            q = tuple(decays[r] * (q[r] + s[r]) for r in range(half))
            s = tuple(decays[r] * s[r] + value for r in range(half))
            p = tuple(p[r] + grad * s[r] for r in range(half))
            l = tuple(l[r] + grad * q[r] for r in range(half))
            terms = [weights[r] * s[r] for r in range(half)]
            while len(terms) > 1:
                terms = [terms[k] + terms[k + 1] for k in range(0, len(terms), 2)]
            answer = terms[0] if base == 0 else at_step(full, n) + terms[0]
            full[pl.ds(n, CHUNKS, stride=STEPS), :] = answer
            return s, q, p, l

        s, q, p, l = lax.fori_loop(0, STEPS, ahead, ((zero,) * half,) * 4, unroll=4)
        s_end += s
        q_end += q
        plain += p
        slope += l
    entries = chunk_entries(s_end, power, False)
    exits = chunk_entries(z_end, power, True)
    back, back_steps = chunk_weights(power, True)
    front, front_steps = chunk_weights(power, False)
    for r in range(MODES):
        a = spread(decay, r)
        a_step = a * spread(power[0], r)
        one = plain[r] + entries[r] * a * z_end[r]
        two = (
            slope[r]
            + float(STEPS) * a_step * entries[r] * exits[r]
            + a * (entries[r] * zq_end[r] + exits[r] * (q_end[r] + s_end[r]))
        )
        back_r, front_r = back(r), front(r)
        rows = (
            one,
            two,
            back_r * z_end[r],
            back_r * (zq_end[r] + back_steps * z_end[r]),
            front_r * (q_end[r] + s_end[r] + front_steps * s_end[r]),
        )
        for kind, value in enumerate(rows):
            place = kind * MODES + r
            sums_out[place : place + 1, :] = jnp.sum(value, 0, keepdims=True)
    y_out[...] = full[...]
    for r in range(MODES):
        entry_out[r] = entries[r]


def kernel_spectrum(forward, filt, copies):
    parts = split_spectrum(spectrum(forward[:, 0:TAPS], filt[...]))
    return [jnp.concatenate([part] * copies, 1) if copies > 1 else part for part in parts]


def local_taps(gco, filt, k_one, v_one, med, before, forward, low, grad_out, taps_out, ext, halo):
    second = gco[TAPS:, :]
    pieces = jnp.concatenate(
        [gco[...], jnp.concatenate([second, jnp.zeros(second.shape, BF16)], 0)], 1
    )
    win = spectrum(forward[...], pieces)
    ker_re, ker_alt, ker_im = kernel_spectrum(forward, filt, 2)
    re, im = win[:TAPS], win[TAPS:]
    spec = jnp.concatenate([re * ker_re + im * ker_im, im * ker_alt - re * ker_im], 0)
    answer = from_spectrum(low[...], spec)
    grad_prod = jnp.concatenate([answer[:, :LANES], answer[:, LANES:]], 0)
    grad_out[...] = grad_prod
    halo[...] = f32_of(before[...])
    taps_out[...] = jnp.zeros(taps_out.shape, F32)
    for place, other in enumerate((v_one, k_one)):
        extend(ext, halo[TAPS + 2 + 2 * place : TAPS + 4 + 2 * place, :], f32_of(med[place + 1]))
        store_tap_sums(taps_out, 3 * place, grad_prod * f32_of(other[...]), ext)


def answer_kernel(me, sg, pair, other, rate, weight, y_loc, inside, q_two, cot, sums, zin, lng, before, tap_rows, after, filt, k_one, v_one, med, forward, low,
                  mixed_out, gq2_out, res_out, row_out, exit_out, late_out, ext, halo, full, rows):
    rates = rate[...]
    entry = entry_state(sg, f32_of(other[0:MODES, :]), rates, me[0], False)
    full[...] = y_loc[...]
    add_entry(full, rates, weight[...], entry, False, inside)
    conv = rounded(full[...])
    grad_out = f32_of(cot[...])
    mixed_out[...] = (f32_of(q_two[...]) * conv).astype(BF16)
    grad_q_two = grad_out * conv
    gq2_out[...] = grad_q_two
    decay = jnp.exp(-rates)
    exit_out[...] = jnp.exp(rates * float(-ROWS)) * entry + f32_of(pair[0:MODES, :])
    plain = sums[0:MODES, :] + entry * decay * sums[2 * MODES : 3 * MODES, :]
    slope = (
        sums[MODES : 2 * MODES, :]
        + float(ROWS) * jnp.exp(rates * float(-ROWS - 1)) * entry * zin[...]
        + decay * (entry * sums[3 * MODES : 4 * MODES, :] + zin[...] * sums[4 * MODES :, :])
    )
    res_out[0:MODES, :] = (jnp.sqrt(2.0 * rates) * plain).astype(BF16)
    res_out[MODES:, :] = (weight[...] * (0.5 * plain - rates * slope)).astype(BF16)
    added = f32_of(sg[0])
    for device in range(1, sg.shape[0]):
        added = added + f32_of(sg[device])
    rows[0:8, :] = added[MODES : MODES + 8]
    rows[SHARE : SHARE + 6, :] = tap_rows[0:6, :]
    win = spectrum(forward[:, TAPS:], after[0:TAPS, :])
    ker_re, ker_alt, ker_im = kernel_spectrum(forward, filt, 1)
    re, im = win[:TAPS], win[TAPS:]
    spec = jnp.concatenate([re * ker_re + im * ker_im, im * ker_alt - re * ker_im], 0)
    late = from_spectrum(low[...], spec)
    late_out[...] = late
    for place, other in enumerate((v_one, k_one)):
        ext[0:ROWS, :] = f32_of(med[place + 1])
        grad = late * f32_of(other[TAPS:, :])
        for shift in range(3):
            row = SHARE + 3 * place + shift
            rows[row : row + 1, :] += jnp.sum(grad * ext[TAPS - shift : ROWS - shift, :], 0, keepdims=True)
    halo[...] = f32_of(before[TAPS:HALO, :])
    extend(ext, halo[6:8, :], f32_of(lng[0]))
    store_tap_sums(rows, SHARE + 6, grad_q_two, ext)
    row_out[...] = rows[...].astype(BF16)


def input_kernel(gq1, gpo, late, gq2, gk2, k_one, v_one, after, leave, rate, weight, mtaps, ltaps,
                 med_out, lng_out, ext, tail, nxt):
    tail[...] = f32_of(after[TAPS:HALO, :])
    grad_prod = jnp.concatenate([gpo[0:TAPS, :], gpo[TAPS:, :] + late[...]], 0)
    state = leave[...]
    decay = jnp.exp(-rate[...])
    for step in range(2):
        state = decay * state + tail[8 + step : 9 + step, :]
        value = rounded(jnp.sum(weight[...] * state, 0, keepdims=True))
        nxt[step : step + 1, :] = value * tail[10 + step : 11 + step, :]

    def back(grad, following, taps):
        ext[0:ROWS, :] = grad
        ext[ROWS : ROWS + 2, :] = following
        return (
            taps[0:1] * ext[0:ROWS, :] + taps[1:2] * ext[1 : ROWS + 1, :] + taps[2:3] * ext[2 : ROWS + 2, :]
        ).astype(BF16)

    med_out[0] = back(gq1[...], tail[0:2, :], mtaps[0])
    med_out[1] = back(grad_prod * f32_of(v_one[...]), tail[2:4, :], mtaps[1])
    med_out[2] = back(grad_prod * f32_of(k_one[...]), tail[4:6, :], mtaps[2])
    lng_out[0] = back(gq2[...], nxt[0:2, :], ltaps[0])
    lng_out[1] = back(gk2[...], tail[6:8, :], ltaps[1])


def last_kernel(me, every, mine, partner, slot_out, slot):
    first = me[0] % 2 == 0
    ours, others = f32_of(every[...]), f32_of(partner[...])
    slot[...] = jnp.zeros(slot.shape, F32)
    slot[0:SHARE, :] = jnp.where(first, ours[0:SHARE], others[0:SHARE])
    slot[SHARE : 2 * SHARE, :] = jnp.where(first, others[0:SHARE], ours[0:SHARE])
    slot[2 * SHARE : 2 * SHARE + 9, :] = ours[SHARE : SHARE + 9] + others[SHARE : SHARE + 9]
    own = f32_of(mine[...]) + others[MODES:]
    for pair in range(PAIRS):
        slot[2 * SHARE + 9 : 2 * SHARE + 10, :] = own[pair : pair + 1]
        slot_out[pair] = slot[...].astype(BF16)


def finish_kernel(last, mtap_out, ltap_out, filt_out, gain_out, res_out, log_out, f_all, block):
    added = jnp.zeros((last.shape[1], LANES), F32)
    for pair in range(PAIRS):
        piece = f32_of(last[pair])
        f_all[SHARE * pair : SHARE * pair + 8, :] = piece[0:8]
        added = added + piece
    for pair in range(PAIRS):
        start = HALF + SHARE * pair
        f_all[start : start + 8, :] = f32_of(last[pair])[SHARE : SHARE + 8]
    filt_out[...] = f_all[0:TAPS, :]
    gain_out[...] = f_all[TAPS : TAPS + 1, :]
    for shift in range(3):
        mtap_out[shift, 0:1, :] = f_all[TAPS + 1 + shift : TAPS + 2 + shift, :]
        ltap_out[shift, 1:2, :] = f_all[TAPS + 4 + shift : TAPS + 5 + shift, :]
        mtap_out[shift, 1:2, :] = added[2 * SHARE + shift : 2 * SHARE + 1 + shift]
        mtap_out[shift, 2:3, :] = added[2 * SHARE + 3 + shift : 2 * SHARE + 4 + shift]
        ltap_out[shift, 0:1, :] = added[2 * SHARE + 6 + shift : 2 * SHARE + 7 + shift]
    lane = lax.broadcasted_iota(jnp.int32, (MODES, LANES), 1)
    row = lax.broadcasted_iota(jnp.int32, (MODES, LANES), 0)
    picked = jnp.where(lane % MODES == row, added[2 * SHARE + 9 : 2 * SHARE + 10], 0.0)
    goal = (row == lane // MODES + 8 * (block % 2)).astype(F32)
    part = lax.dot_general(
        picked, goal, (((1,), (1,)), ((), ())), precision=precise, preferred_element_type=F32
    )

    target = res_out if block < 2 else log_out
    if block % 2 == 0:
        target[...] = part
    else:
        target[...] += part


def view_of(ref, kind, block):
    if kind == "lane":
        return ref.at[(slice(None),) * (len(ref.shape) - 1) + (pl.ds(LANES * block, LANES),)]
    if kind == "source":
        return ref.at[pl.ds(8 * block, 8)]
    return ref


def spec_of(shape, kind):
    lead = shape[:-1]
    if kind == "lane":
        return pl.BlockSpec(lead + (LANES,), lambda l: (0,) * len(lead) + (l,))
    if kind == "whole":
        return pl.BlockSpec(shape, lambda l: (0,) * len(shape))
    return pl.BlockSpec(memory_space=pltpu.SMEM)


def run(kernel, name, width, inputs, outputs, scratch, limit=63, whole=False, blocks=False, grid=False):
    arrays = [array for array, _ in inputs]
    kinds = [kind for _, kind in inputs] + [kind for _, _, kind in outputs]

    def body(*refs):
        if whole or grid:
            return kernel(*refs)
        for block in range(width // LANES):
            views = [view_of(ref, kind, block) for ref, kind in zip(refs, kinds)]
            extra = {"block": block} if blocks else {}
            kernel(*views, *refs[len(kinds) :], **extra)

    moved = sum(a.size * a.dtype.itemsize for a in arrays)
    vmem = pl.BlockSpec(memory_space=pltpu.VMEM)
    if grid:
        places = {
            "grid": (width // LANES,),
            "in_specs": [spec_of(a.shape, kind) for a, kind in inputs],
            "out_specs": [spec_of(shape, kind) for shape, _, kind in outputs],
        }
    else:
        places = {
            "in_specs": [
                pl.BlockSpec(memory_space=pltpu.SMEM) if kind == "scalar" else vmem for _, kind in inputs
            ],
            "out_specs": [vmem for _ in outputs],
        }
    return pl.pallas_call(
        body,
        **places,
        out_shape=[jax.ShapeDtypeStruct(shape, dtype) for shape, dtype, _ in outputs],
        scratch_shapes=[pltpu.VMEM(shape, F32) for shape in scratch],
        compiler_params=pltpu.CompilerParams(vmem_limit_bytes=limit * 1024 * 1024),
        cost_estimate=pl.CostEstimate(flops=1000000, bytes_accessed=moved, transcendentals=0),
        name=name,
    )(*arrays)


def passed_along(array, axis, by):
    count = lax.axis_size(axis)
    pairs = [(i, i + by) for i in range(count) if 0 <= i + by < count]
    return lax.ppermute(array, axis, pairs)


def exchanged(array):
    return lax.ppermute(array, "ctx", [(i, i ^ 1) for i in range(lax.axis_size("ctx"))])


def in_plane(array):
    groups = [[2 * p + z for p in range(PAIRS)] for z in range(2)]
    return lax.all_to_all(array, "ctx", split_axis=0, concat_axis=0, tiled=True, axis_index_groups=groups)


def swap(array, axis):
    return lax.all_to_all(array, axis, split_axis=0, concat_axis=0, tiled=True)


def on_device(medium_input, long_input, medium_taps, long_taps, medium_filter, norm_gain, long_residue, long_log_decay, cotangent):
    width = cotangent.shape[1]
    count = lax.axis_size("ctx")
    me = lax.axis_index("ctx").astype(jnp.int32).reshape(1)
    forward, low, top = (jnp.asarray(table) for table in fourier_matrices())
    med = jnp.transpose(medium_input, (1, 0, 2))
    lng = jnp.transpose(long_input, (1, 0, 2))
    mtaps = jnp.transpose(medium_taps, (1, 0, 2))
    ltaps = jnp.transpose(long_taps, (1, 0, 2))
    gain = norm_gain.reshape(1, width)
    filt = medium_filter
    ext = (ROWS + 8, LANES)
    halo = (HALO, LANES)
    wide = (WIDE, width)
    full = (ROWS, LANES)
    rows = (MODES, LANES)
    plane = (ROWS, width)
    modes = (MODES, width)

    mine = jnp.pad(jnp.concatenate([long_log_decay, long_residue], 1), ((0, 0), (0, LANES - 2 * MODES)))
    packed = swap(jnp.broadcast_to(mine[None], (count,) + mine.shape), "ctx")

    ends = jnp.transpose(long_input[ROWS - 2 :].astype(F32), (1, 0, 2)).reshape(4, width)
    (tail,) = run(
        tail_kernel, "tail", width, [(med, "lane"), (ends, "lane"), (mtaps, "lane")],
        [((HALO, width), BF16, "lane")], [ext, rows], limit=16,
    )
    before = passed_along(tail, "ctx", 1)

    rate, weight, q_two, k_two, gconv, z_all, z_ends = run(
        long_kernel, "long", width,
        [(packed, "source"), (before, "lane"), (lng, "lane"), (ltaps, "lane"), (cotangent, "lane")],
        [(modes, F32, "lane"), (modes, F32, "lane"), (plane, BF16, "lane"), (plane, BF16, "lane"), (plane, BF16, "lane"), (modes, BF16, "lane"), ((MODES, CHUNKS, width), F32, "lane")],
        [ext, halo, full, rows],
    )
    z_other = exchanged(z_all)
    prod, q_one, k_one, v_one, conv, gated, square = run(
        medium_kernel, "medium", width,
        [(med, "lane"), (before, "lane"), (mtaps, "lane"), (filt, "lane"), (forward, "whole"), (top, "whole")],
        [(wide, BF16, "lane"), (plane, BF16, "lane"), (plane, BF16, "lane"), (plane, BF16, "lane"), (plane, F32, "lane"), (plane, F32, "lane"), ((8, ROWS), F32, "whole")],
        [ext, halo], blocks=True,
    )
    z_other, square = lax.optimization_barrier((z_other, square))
    (z_pairs,) = run(
        join_kernel, "join", width, [(me, "scalar"), (z_all, "lane"), (z_other, "lane"), (rate, "lane")],
        [((PAIRS,) + modes, BF16, "lane")], [], whole=True,
    )
    zg = in_plane(z_pairs)
    (y_back,) = run(
        back_kernel, "back", width,
        [(gconv, "lane"), (rate, "lane"), (weight, "lane"), (z_ends, "lane")],
        [(plane, F32, "lane")], [full, full],
    )
    grad_prod, zin, inner = run(
        inner_kernel, "inner", width,
        [(me, "scalar"), (zg, "lane"), (z_other, "lane"), (rate, "lane"), (weight, "lane"), (y_back, "lane"), (k_two, "lane"), (gated, "lane"), (gain, "lane"), (square, "whole")],
        [(plane, BF16, "lane"), (modes, F32, "lane"), ((8, 1, 2 * ROWS), F32, "whole")],
        [full, (8, ROWS)], grid=True,
    )
    sums = swap(inner, "tp")
    later, _ = lax.optimization_barrier((gconv, inner))
    (ends_back,) = run(
        behind_kernel, "behind", width, [(later, "lane"), (rate, "lane")],
        [((2 * MODES, CHUNKS, width), F32, "lane")], [full],
    )
    sums, ends_back = lax.optimization_barrier((sums, ends_back))

    x, gco, gq1, gk2, edge, pair, keep = run(
        norm_kernel, "norm", width,
        [(me, "scalar"), (sums, "whole"), (gated, "lane"), (conv, "lane"), (q_one, "lane"), (k_one, "lane"), (v_one, "lane"), (k_two, "lane"), (grad_prod, "lane"), (gain, "lane"), (filt, "lane"), (cotangent, "lane"), (prod, "lane"), (med, "lane"), (lng, "lane"), (before, "lane"), (rate, "lane"), (forward, "whole"), (low, "whole")],
        [(plane, BF16, "lane"), (plane, BF16, "lane"), (plane, F32, "lane"), (plane, F32, "lane"), ((HALO, width), BF16, "lane"), ((MODES + HALF, width), BF16, "lane"), ((HALF, width), F32, "lane")],
        [full, rows, ext, halo, (2 * HALF, LANES)], grid=True,
    )
    other = exchanged(pair)
    gpo, tap_rows = run(
        local_taps, "taps", width,
        [(gco, "lane"), (filt, "lane"), (k_one, "lane"), (v_one, "lane"), (med, "lane"), (before, "lane"), (forward, "whole"), (low, "whole")],
        [(plane, F32, "lane"), ((8, width), F32, "lane")], [ext, halo],
    )
    edge, tap_rows = lax.optimization_barrier((edge, tap_rows))
    after = passed_along(edge, "ctx", -1)
    other, tap_rows = lax.optimization_barrier((other, tap_rows))
    (sent,) = run(
        share_kernel, "share", width,
        [(me, "scalar"), (pair, "lane"), (other, "lane"), (keep, "lane"), (rate, "lane")],
        [((PAIRS, MODES + 8, width), BF16, "lane")], [(HALF + 8, width), (MODES + 8, width)], whole=True,
    )
    got = in_plane(sent)

    y_front, mode_sums, inside = run(
        modes_kernel, "modes", width,
        [(x, "lane"), (gconv, "lane"), (rate, "lane"), (weight, "lane"), (ends_back, "lane")],
        [(plane, F32, "lane"), ((5 * MODES, width), F32, "lane"), ((MODES, CHUNKS, width), F32, "lane")], [full, full, full], grid=True,
    )
    mixed, gq2, res, every, leave, late = run(
        answer_kernel, "answer", width,
        [(me, "scalar"), (got, "lane"), (pair, "lane"), (other, "lane"), (rate, "lane"), (weight, "lane"), (y_front, "lane"), (inside, "lane"), (q_two, "lane"), (cotangent, "lane"), (mode_sums, "lane"), (zin, "lane"), (lng, "lane"), (before, "lane"), (tap_rows, "lane"), (after, "lane"), (filt, "lane"), (k_one, "lane"), (v_one, "lane"), (med, "lane"), (forward, "whole"), (low, "whole")],
        [(plane, BF16, "lane"), (plane, F32, "lane"), ((2 * MODES, width), BF16, "lane"), ((MODES, width), BF16, "lane"), (modes, F32, "lane"), ((TAPS, width), F32, "lane")],
        [ext, rows, full, rows], grid=True,
    )
    own = res.reshape(2 * MODES, PAIRS, 2, MODES).transpose(2, 1, 0, 3).reshape(2, PAIRS, width)
    second = me[0] % 2
    mine = lax.dynamic_index_in_dim(own, second, 0, keepdims=False)
    theirs = lax.dynamic_index_in_dim(own, 1 - second, 0, keepdims=False)
    partner = exchanged(jnp.concatenate([every, theirs], 0))
    (slots,) = run(
        last_kernel, "last", width,
        [(me, "scalar"), (every, "lane"), (mine, "lane"), (partner, "lane")],
        [((PAIRS, 24, width), BF16, "lane")], [(24, width)], whole=True,
    )
    last = in_plane(slots)

    grad_med, grad_lng = run(
        input_kernel, "inputs", width,
        [(gq1, "lane"), (gpo, "lane"), (late, "lane"), (gq2, "lane"), (gk2, "lane"), (k_one, "lane"), (v_one, "lane"), (after, "lane"), (leave, "lane"), (rate, "lane"), (weight, "lane"), (mtaps, "lane"), (ltaps, "lane")],
        [((3, ROWS, width), BF16, "lane"), ((2, ROWS, width), BF16, "lane")],
        [ext, rows, (8, LANES)],
    )
    taps_medium, taps_long, grad_filter, gain_total, grad_residue, grad_log = run(
        finish_kernel, "finish", width, [(last, "lane")],
        [((3, 3, width), F32, "lane"), ((3, 2, width), F32, "lane"), ((TAPS, width), F32, "lane"), ((1, width), F32, "lane"), ((MODES, MODES), F32, "whole"), ((MODES, MODES), F32, "whole")],
        [(SHARE * count + 8, LANES)], limit=16, blocks=True,
    )
    return (
        mixed,
        jnp.transpose(grad_med, (1, 0, 2)),
        jnp.transpose(grad_lng, (1, 0, 2)),
        taps_medium,
        taps_long,
        grad_filter,
        gain_total.reshape(width),
        grad_residue,
        grad_log,
    )


def solution(mesh):
    return jax.shard_map(
        on_device,
        mesh=mesh,
        in_specs=(
            P("ctx", None, "tp"),
            P("ctx", None, "tp"),
            P(None, None, "tp"),
            P(None, None, "tp"),
            P(None, "tp"),
            P("tp"),
            P(("tp", "ctx"), None),
            P(("tp", "ctx"), None),
            P("ctx", "tp"),
        ),
        out_specs=(
            P("ctx", "tp"),
            P("ctx", None, "tp"),
            P("ctx", None, "tp"),
            P(None, None, "tp"),
            P(None, None, "tp"),
            P(None, "tp"),
            P("tp"),
            P(("tp", "ctx"), None),
            P(("tp", "ctx"), None),
        ),
        check_vma=False,
    )
```
